32 devices in a mesh: space: 16 (over z, x, core), tm: 2 (over y).
Axes of the slice: x: 2, y: 2, z: 4, core: 2. Of those that a mesh axis runs over, the one named last changes fastest.
Arguments:
- query_key: bfloat16 [1, 16384, 64], P(None, 'space'), may hold values from -1.5 to 8
- selection: bfloat16 [1, 16384, 64], P(None, 'space'), may hold values from 0.19921875 to 1
- memory_key: bfloat16 [8, 16384, 64], P('tm', 'space'), may hold values from -1.5 to 1.5
- shrinkage: bfloat16 [8, 16384], P('tm', 'space'), may hold values from 1 to 4
- memory_value: bfloat16 [8, 16384, 512], P('tm', 'space'), may hold values from -6 to 6
- block_list: int32 [128, 6], P('space'), may hold values from 0 to 11, as said below
- block_count: int32 [128], P('space'), may hold values from 1 to 6, as said below
Outputs:
- readout: bfloat16 [1, 16384, 512], P(None, 'space')
The draws below stay inside these ranges and needn't reach their ends.
Inputs may be any that keep to these rules, and one draw needn't show every extreme that they name: `block_list`: entries of a row are distinct; rows of the first tile name no block under 2, rows of the last tile none of 10 or above. `block_count`: the first block of every tile uses all 6 listed blocks.
All inputs are finite; a program needn't handle non-finite values.
Results may differ from the reference program's by a relative error of at most 0.0061.
Values may be sent and summed in bfloat16 or wider, within the bound.
No kernel may reach another device: no remote copies, remote signals or barrier semaphores. Data moves between devices by JAX's collectives and lax.ppermute only.
A program may use at most 128 MiB of HBM per device.

```python
import math
import jax
import jax.numpy as jnp
from jax import lax

CK = 64
CV = 512
BS = 128
W = 2
NL = 6
FD = 4
Q = 1
NBLK = 8
NPIX = 16384
QBLK = 128
MEM = 8
WIN = 12
N_SPACE = 16
N_TM = 2


def draw_query_key(key, part):
    base_part = jnp.clip(0.25 * jax.random.normal(key, (Q, NPIX, CK), jnp.float32), -1.5, 1.5)
    return base_part.astype(jnp.bfloat16)


def draw_block_list(key, part):
    tile_of = (jnp.arange(QBLK, dtype=jnp.int32) // NBLK)[:, None]
    slot_of = jnp.arange(WIN, dtype=jnp.int32)[None, :]
    random_part = jax.random.randint(key, (QBLK, WIN), 0, 2 ** 20)
    scores = random_part * WIN + slot_of
    barred = (tile_of == 0) & (slot_of < W) | (tile_of == N_SPACE - 1) & (slot_of >= W + NBLK)
    scores = scores + jnp.where(barred, 2 ** 28, 0)
    ignored, chosen = lax.top_k(-scores, NL)
    return chosen.astype(jnp.int32)


def draw_block_count(key, part):
    counts = jax.random.randint(key, (QBLK,), 1, NL + 1)
    leading = jnp.arange(QBLK, dtype=jnp.int32) % NBLK == 0
    return jnp.where(leading, NL, counts).astype(jnp.int32)


def shard_levels(own_key, dims, shards, low, high):
    level = 1.0
    for position, blocks in shards:
        draws = jax.random.uniform(jax.random.fold_in(jax.random.fold_in(own_key, 6), position), (blocks,), jnp.float32, low / len(shards), high / len(shards))
        level = level * jnp.repeat(jnp.exp(draws), dims[position] // blocks).reshape((-1,) + (1,) * (len(dims) - 1 - position))
    return level


def normal_values(key, extent, spread, bound, shards=(), kind=jnp.bfloat16):
    values = jax.random.normal(key, extent, jnp.float32) * spread
    if len(shards) > 0:
        values = shard_levels(key, extent, shards, -0.22, 0.18) * values
    return jnp.clip(values, min=-bound, max=bound).astype(kind)


def setup_inputs(seed: int = 0) -> dict:
    streams_of = jax.random.split(jax.random.key(seed), 8)
    query_key = draw_query_key(jax.random.fold_in(streams_of[7], 71), 0)
    selection = jnp.clip(0.19921875 + 0.80078125 * jax.random.uniform(streams_of[1], (Q, NPIX, CK), jnp.float32) ** shard_levels(streams_of[1], (Q, NPIX, CK), ((1, 16),), -0.2, 0.2), 0.19921875, 1.0).astype(jnp.bfloat16)
    memory_key = normal_values(streams_of[2], (MEM, NPIX, CK), 0.25, 1.5, ((0, 2), (1, 16)))
    shrinkage = jnp.clip(jnp.exp(math.log(4.0) - 1.3862944 * jax.random.uniform(streams_of[3], (MEM, NPIX), jnp.float32) ** shard_levels(streams_of[3], (MEM, NPIX), ((0, 2), (1, 16)), -0.2, 0.2)), 1.0, 4.0).astype(jnp.bfloat16)
    memory_value = normal_values(streams_of[4], (MEM, NPIX, CV), 1.0, 6.0, ((0, 2), (1, 16)))
    block_list = draw_block_list(jax.random.fold_in(streams_of[7], 71), 0)
    block_count = draw_block_count(jax.random.fold_in(streams_of[7], 71), 0)
    return {"query_key": query_key, "selection": selection, "memory_key": memory_key, "shrinkage": shrinkage, "memory_value": memory_value, "block_list": block_list, "block_count": block_count}


def reference(query_key, selection, memory_key, shrinkage, memory_value, block_list, block_count):
    score_scale = 1.0 / math.sqrt(CK)
    query_f = query_key.astype(jnp.float32)
    select_f = selection.astype(jnp.float32)
    query_sel = lax.optimization_barrier((2.0 * query_f * select_f).astype(jnp.bfloat16))
    self_term = lax.optimization_barrier(jnp.sum(select_f * query_f * query_f, axis=-1))
    key_square = lax.optimization_barrier((memory_key.astype(jnp.float32) ** 2).astype(jnp.bfloat16))
    key_blocks = memory_key.reshape(MEM, QBLK, BS, CK)
    square_blocks = key_square.reshape(MEM, QBLK, BS, CK)
    value_blocks = memory_value.reshape(MEM, QBLK, BS, CV)
    shrink_blocks = shrinkage.reshape(MEM, QBLK, BS)
    query_rows = query_sel.reshape(Q, QBLK, BS, CK).transpose(1, 0, 2, 3)
    select_rows = selection.reshape(Q, QBLK, BS, CK).transpose(1, 0, 2, 3)
    self_rows = self_term.reshape(Q, QBLK, BS).transpose(1, 0, 2)
    block_ids = jnp.arange(QBLK, dtype=jnp.int32)

    def one_block(inputs):
        block_id, query_blk, select_blk, self_blk, listed, live_count = inputs
        global_ids = (block_id // NBLK * NBLK + listed - W).astype(jnp.int32)
        squares = jnp.take(square_blocks, global_ids, axis=1).astype(jnp.float32)
        key_rows = jnp.take(key_blocks, global_ids, axis=1).astype(jnp.float32)
        shrink = jnp.take(shrink_blocks, global_ids, axis=1).astype(jnp.float32)
        values = jnp.take(value_blocks, global_ids, axis=1).astype(jnp.float32)
        quad_term = jnp.einsum('qrc,mjnc->qrmjn', select_blk.astype(jnp.float32), squares)
        cross_term = jnp.einsum('qrc,mjnc->qrmjn', query_blk.astype(jnp.float32), key_rows)
        scores = -shrink[None, None] * (quad_term - cross_term + self_blk[:, :, None, None, None]) * score_scale
        scores = scores.reshape(Q, BS, N_TM, FD, NL, BS)
        usable = (jnp.arange(NL, dtype=jnp.int32) < live_count)[None, None, None, None, :, None]
        group_top = lax.optimization_barrier(jnp.max(jnp.where(usable, scores, -jnp.inf), axis=(3, 4, 5)))
        shifted = scores - group_top[:, :, :, None, None, None]
        weights = jnp.where(usable, jnp.exp(shifted), jnp.zeros_like(scores))
        group_total = lax.optimization_barrier(jnp.sum(weights, axis=(3, 4, 5)))
        rounded = lax.optimization_barrier(weights.astype(jnp.bfloat16)).astype(jnp.float32)
        grouped_values = values.reshape(N_TM, FD, NL, BS, CV)
        group_sum = jnp.einsum('qrgfjn,gfjnv->qrgv', rounded, grouped_values)
        row_top = lax.optimization_barrier(jnp.max(group_top, axis=2, keepdims=True))
        factor = jnp.exp(group_top - row_top)
        summed = lax.optimization_barrier(jnp.sum(factor[:, :, :, None] * group_sum, axis=2))
        row_total = lax.optimization_barrier(jnp.sum(factor * group_total, axis=2))
        return (summed / row_total[:, :, None]).astype(jnp.bfloat16)
    blocks = lax.map(one_block, (block_ids, query_rows, select_rows, self_rows, block_list, block_count))
    return blocks.transpose(1, 0, 2, 3).reshape(Q, NPIX, CV)
```

```python
import functools
import math

import jax
import jax.numpy as jnp
from jax import lax
from jax.experimental import pallas as pl
from jax.experimental.pallas import tpu as pltpu
from jax.sharding import PartitionSpec as P

BS = 128
W = 2
LANES = 128
EDGE = W * BS
NONE = -1e30
OWN_AT, HALO_AT, COUNT_AT = 0, 64, 128
F32, BF16 = jnp.float32, jnp.bfloat16

VMEM = pl.BlockSpec(memory_space=pltpu.VMEM)
SMEM = pl.BlockSpec(memory_space=pltpu.SMEM)
HBM = pl.BlockSpec(memory_space=pl.ANY)


def params(mib):
    return pltpu.CompilerParams(vmem_limit_bytes=mib * 1024 * 1024)


def nt_dot(a, b):
    return lax.dot_general(a, b, (((1,), (1,)), ((), ())), preferred_element_type=F32)


def lane_tiles(x):
    return [x[:, i * LANES : (i + 1) * LANES] for i in range(x.shape[1] // LANES)]


def wide(x, times):
    return jnp.concatenate([x] * times, axis=1)


def lists_and_edges(
    sizes, list_ref, count_ref, key_ref, shrink_ref, value_ref, pairs_ref, chip_ref, link_ref, key_sc, shr_sc, sems
):
    frames, pixels, n_blocks, n_listed, key_width, value_width = sizes
    odd = lax.rem(lax.axis_index("space"), 2)
    rows = frames * EDGE
    starts = [
        pl.multiple_of((1 - odd) * (pixels - EDGE), EDGE),
        pl.multiple_of(odd * (pixels - EDGE), EDGE),
    ]
    copies = []
    for e in range(W):
        for f in range(frames):
            at = (e * frames + f) * BS
            copies.append(
                pltpu.make_async_copy(
                    value_ref.at[f, pl.ds(starts[0] + e * BS, BS), :],
                    chip_ref.at[pl.ds(at, BS), :],
                    sems.at[0, e * frames + f],
                )
            )
            copies.append(
                pltpu.make_async_copy(
                    value_ref.at[f, pl.ds(starts[1] + e * BS, BS), pl.ds(0, LANES)],
                    link_ref.at[pl.ds(at, BS), :],
                    sems.at[1, e * frames + f],
                )
            )
    for copy in copies:
        copy.start()
    last = []
    for side in range(2):
        for f in range(frames):
            blocks = [key_ref[f, pl.ds(starts[side] + e * BS, BS), :] for e in range(W)]
            key_sc[side, f * BS : (f + 1) * BS, :] = jnp.concatenate(blocks, axis=1)
        edge = shrink_ref[:, pl.ds(starts[side], EDGE)].astype(F32)
        rows_e = [edge[:, e * BS : (e + 1) * BS] for e in range(W)]
        pad = jnp.zeros((16 - W * frames, LANES), F32)
        key_sc[side, frames * BS :, :] = jnp.concatenate(rows_e + [pad], axis=0).astype(BF16)
    key_rows = frames * BS + 16
    if True:
        copy = pltpu.make_async_copy(key_sc.at[1], link_ref.at[pl.ds(rows, key_rows), :], sems.at[1, W * frames])
        copy.start()
        last.append(copy)
        for i in range(4):
            part = key_rows // 4 // 16 * 16
            size = part if i < 3 else key_rows - 3 * part
            copy = pltpu.make_async_copy(
                key_sc.at[0, pl.ds(i * part, size), :],
                chip_ref.at[pl.ds(rows, size), pl.ds(i * LANES, LANES)],
                sems.at[0, W * frames + i],
            )
            copy.start()
            last.append(copy)

    def block(b, carry):
        live = count_ref[b]
        for j in range(n_listed):
            n_own, n_halo = carry
            l = list_ref[b, j]
            ok = j < live
            inside = (l >= W) & (l < W + n_blocks)
            right = jnp.where(l >= W + n_blocks, 1, 0)
            e = jnp.where(right == 1, l - (W + n_blocks), l)
            over_link = jnp.where(right == odd, 1, 0)
            pairs_ref[OWN_AT + n_own] = b * n_blocks + jnp.clip(l - W, 0, n_blocks - 1)
            pairs_ref[HALO_AT + n_halo] = b * 4 + over_link * W + jnp.clip(e, 0, W - 1)
            carry = (
                n_own + jnp.where(ok & inside, 1, 0),
                n_halo + jnp.where(ok & jnp.logical_not(inside), 1, 0),
            )
        return carry

    n_own, n_halo = lax.fori_loop(0, n_blocks, block, (0, 0))
    pairs_ref[OWN_AT + n_own] = n_blocks * n_blocks
    pairs_ref[HALO_AT + n_halo] = n_blocks * 4
    pairs_ref[COUNT_AT] = n_own
    pairs_ref[COUNT_AT + 1] = n_halo
    for copy in copies + last:
        copy.wait()


def edge_chunks(sizes, n_chunks, value_ref, *refs):
    frames, pixels = sizes[:2]
    outs, sems = refs[:-1], refs[-1]
    odd = lax.rem(lax.axis_index("space"), 2)
    start = pl.multiple_of(odd * (pixels - EDGE), EDGE)
    copies = []
    for c, out in enumerate(outs):
        for e in range(W):
            for f in range(frames):
                copies.append(
                    pltpu.make_async_copy(
                        value_ref.at[f, pl.ds(start + e * BS, BS), pl.ds((c + 1) * LANES, LANES)],
                        out.at[pl.ds((e * frames + f) * BS, BS), :],
                        sems.at[c, e * frames + f],
                    )
                )
    for copy in copies:
        copy.start()
    for copy in copies:
        copy.wait()


def paired(count, body):
    def step(i, carry):
        body(2 * i)
        body(2 * i + 1)
        return carry

    lax.fori_loop(0, (count + 1) // 2, step, 0)


def own_part(
    sizes, pairs_ref, query_ref, select_ref, key_ref, shrink_ref, value_ref,
    acc_ref, top_ref, total_ref, cat_ref, self_ref,
    keys_sc, shr_sc, score_sc, value_sc, sem,
):
    frames, pixels, n_blocks, n_listed, key_width, value_width = sizes
    cols = frames * BS
    bits = int(math.log2(n_blocks))
    values = pltpu.make_async_copy(value_ref, value_sc, sem)
    values.start()
    scale = -math.log2(math.e) / math.sqrt(key_width)
    for b in range(n_blocks):
        q = query_ref[b * BS : (b + 1) * BS, :].astype(F32)
        s = select_ref[b * BS : (b + 1) * BS, :]
        s_f = s.astype(F32)
        cat_ref[b] = jnp.concatenate([s, (-2.0 * q * s_f).astype(BF16)], axis=1)
        term = jnp.sum(s_f * q * q, axis=1, keepdims=True)
        self_ref[b] = jnp.broadcast_to(term, (BS, LANES))
    cat_ref[n_blocks] = jnp.zeros((BS, 2 * key_width), BF16)
    self_ref[n_blocks] = jnp.zeros((BS, LANES), F32)
    shrink = shrink_ref[...].astype(F32) * scale
    for l in range(n_blocks):
        for f in range(frames):
            k = key_ref[f, l * BS : (l + 1) * BS, :]
            k_f = k.astype(F32)
            keys_sc[l, f * BS : (f + 1) * BS, :] = jnp.concatenate([(k_f * k_f).astype(BF16), k], axis=1)
            shr_sc[l, :, f * BS : (f + 1) * BS] = shrink[f : f + 1, l * BS : (l + 1) * BS]
    top_ref[...] = jnp.full_like(top_ref, NONE)
    total_ref[...] = jnp.zeros_like(total_ref)
    acc_ref[...] = jnp.zeros_like(acc_ref)
    count = pairs_ref[COUNT_AT]

    def score(p):
        code = pairs_ref[OWN_AT + p]
        b, l = code >> bits, code & (n_blocks - 1)
        s = nt_dot(cat_ref[b], keys_sc[l])
        s = (s + wide(self_ref[b], frames)) * shr_sc[l]
        score_sc[p] = s
        top_ref[b] = functools.reduce(jnp.maximum, lane_tiles(s), top_ref[b])

    paired(count, score)
    for b in range(n_blocks):
        top_ref[b] = jnp.broadcast_to(jnp.max(top_ref[b], axis=1, keepdims=True), (BS, LANES))
    values.wait()

    def read(p):
        code = pairs_ref[OWN_AT + p]
        b, l = code >> bits, code & (n_blocks - 1)
        w = jnp.exp2(score_sc[p] - wide(top_ref[b], frames))
        total_ref[b] = functools.reduce(jnp.add, lane_tiles(w), total_ref[b])
        v = value_sc[:, pl.ds(pl.multiple_of(l * BS, BS), BS), :].reshape(cols, value_width)
        acc_ref[b] += jnp.dot(w.astype(BF16), v, preferred_element_type=F32)

    paired(count, read)


def halo_scores(
    sizes, pairs_ref, cat_ref, self_ref, chip_ref, link_ref, own_top_ref, own_total_ref,
    weight_ref, factor_ref, stats_ref,
    keys_sc, shr_sc, score_sc, top_sc, total_sc, weight_sc, sems,
):
    frames, pixels, n_blocks, n_listed, key_width, value_width = sizes
    rows = frames * EDGE
    key_rows = frames * BS + 16
    part = key_rows // 4 // 16 * 16
    scale = -math.log2(math.e) / math.sqrt(key_width)
    chip_parts = [
        chip_ref[: (part if i < 3 else key_rows - 3 * part), i * LANES : (i + 1) * LANES] for i in range(4)
    ]
    packs = [jnp.concatenate(chip_parts, axis=0), link_ref[...]]
    for side in range(2):
        shrink = packs[side][frames * BS :, :].astype(F32) * scale
        for f in range(frames):
            k2 = packs[side][f * BS : (f + 1) * BS, :]
            k2_f = k2.astype(F32)
            q2 = (k2_f * k2_f).astype(BF16)
            for e in range(W):
                lanes = slice(e * key_width, (e + 1) * key_width)
                keys_sc[side * W + e, f * BS : (f + 1) * BS, :] = jnp.concatenate([q2[:, lanes], k2[:, lanes]], axis=1)
                at = e * frames + f
                shr_sc[side * W + e, :, f * BS : (f + 1) * BS] = shrink[at : at + 1, :]
    top_sc[...] = jnp.full_like(top_sc, NONE)
    total_sc[...] = jnp.zeros_like(total_sc)
    count = pairs_ref[COUNT_AT + 1]

    def score(p):
        code = pairs_ref[HALO_AT + p]
        b, h = code >> 2, code & 3
        s = nt_dot(cat_ref[b], keys_sc[h])
        s = (s + wide(self_ref[b], frames)) * shr_sc[h]
        score_sc[p] = s
        top_sc[b] = functools.reduce(jnp.maximum, lane_tiles(s), top_sc[b])

    paired(count, score)
    for b in range(n_blocks):
        own = own_top_ref[b]
        top = jnp.maximum(own, jnp.broadcast_to(jnp.max(top_sc[b], axis=1, keepdims=True), (BS, LANES)))
        top_sc[b] = top
        factor_ref[b] = jnp.exp2(own - top)

    def weigh(p):
        code = pairs_ref[HALO_AT + p]
        b = code >> 2
        w = jnp.exp2(score_sc[p] - wide(top_sc[b], frames))
        total_sc[b] = functools.reduce(jnp.add, lane_tiles(w), total_sc[b])
        weight_sc[p] = w.astype(BF16)
        pltpu.make_async_copy(weight_sc.at[p], weight_ref.at[p], sems.at[p]).start()

    paired(count, weigh)
    for b in range(n_blocks):
        total = jnp.sum(total_sc[b] + own_total_ref[b] * factor_ref[b], axis=1, keepdims=True)
        stats_ref[b : b + 1, :] = jnp.transpose(top_sc[b])[:1, :]
        stats_ref[n_blocks + b : n_blocks + b + 1, :] = jnp.transpose(jnp.broadcast_to(total, (BS, LANES)))[:1, :]

    def drain(p):
        pltpu.make_async_copy(weight_sc.at[p], weight_ref.at[p], sems.at[p]).wait()

    paired(count, drain)


def chunk_sums(sizes, c, pairs_ref, weight_ref, acc_ref, factor_ref, stats_ref, chip_ref, link_ref, out_ref, weight_sc, sum_sc, sems):
    frames, pixels, n_blocks, n_listed, key_width, value_width = sizes
    cols = frames * BS
    count = pairs_ref[COUNT_AT + 1]

    def fetch(p):
        pltpu.make_async_copy(weight_ref.at[p], weight_sc.at[p], sems.at[p]).start()

    paired(count, fetch)
    for b in range(n_blocks):
        sum_sc[b] = acc_ref[b] * factor_ref[b]
    sum_sc[n_blocks] = jnp.zeros((BS, LANES), F32)

    def add(p):
        pltpu.make_async_copy(weight_ref.at[p], weight_sc.at[p], sems.at[p]).wait()
        code = pairs_ref[HALO_AT + p]
        b, h = code >> 2, code & 3
        at = pl.multiple_of((h & (W - 1)) * cols, cols)
        v = jnp.where(h >= W, link_ref[pl.ds(at, cols), :], chip_ref[pl.ds(at, cols), :])
        sum_sc[b] += jnp.dot(weight_sc[p], v, preferred_element_type=F32)

    paired(count, add)
    for b in range(n_blocks):
        out_ref[b * BS : (b + 1) * BS, :] = sum_sc[b].astype(BF16)
    if c == 0:
        rest = stats_ref[...]
        for i in range(3):
            piece = rest.astype(BF16)
            rest = rest - piece.astype(F32)
            out_ref[pixels + i * 2 * n_blocks : pixels + (i + 1) * 2 * n_blocks, :] = piece


def unpack_stats(x, n_blocks):
    n = 2 * n_blocks
    x = x.astype(F32)
    x = (x[:n] + x[n : 2 * n]) + x[2 * n :]
    return x[:n_blocks], x[n_blocks:]


def combine(sizes, n_chunks, *refs):
    frames, pixels, n_blocks = sizes[:3]
    mine, other, out_ref = refs[:n_chunks], refs[n_chunks : 2 * n_chunks], refs[-1]

    def run(first, second):
        top_a, total_a = unpack_stats(first[0][pixels:, :], n_blocks)
        top_b, total_b = unpack_stats(second[0][pixels:, :], n_blocks)
        top = jnp.maximum(top_a, top_b)
        a, b = jnp.exp2(top_a - top), jnp.exp2(top_b - top)
        total = total_a * a + total_b * b
        a, b = a / total, b / total
        for i in range(n_blocks):
            col_a = jnp.transpose(jnp.broadcast_to(a[i : i + 1, :], (BS, LANES)))
            col_b = jnp.transpose(jnp.broadcast_to(b[i : i + 1, :], (BS, LANES)))
            r = slice(i * BS, (i + 1) * BS)
            for c in range(n_chunks):
                x = first[c][r, :].astype(F32) * col_a + second[c][r, :].astype(F32) * col_b
                out_ref[r, c * LANES : (c + 1) * LANES] = x.astype(BF16)

    me = lax.axis_index("tm")

    @pl.when(me == 0)
    def _():
        run(mine, other)

    @pl.when(me != 0)
    def _():
        run(other, mine)


def shards(n_space, n_tm, query_key, selection, memory_key, shrinkage, memory_value, block_list, block_count):
    frames, pixels, key_width = memory_key.shape
    value_width = memory_value.shape[2]
    n_blocks, n_listed = block_list.shape
    sizes = (frames, pixels, n_blocks, n_listed, key_width, value_width)
    n_chunks = value_width // LANES
    rows = frames * EDGE
    key_rows = frames * BS + 16
    chip_key_rows = key_rows - 3 * (key_rows // 4 // 16 * 16)
    max_halo = n_blocks * min(n_listed, 2 * W) + 2
    max_own = n_blocks * n_listed + 2
    struct = jax.ShapeDtypeStruct
    query, select = query_key[0], selection[0]

    pairs, chip_edge, link_edge = pl.pallas_call(
        functools.partial(lists_and_edges, sizes),
        out_shape=(
            struct((256,), jnp.int32),
            struct((rows + chip_key_rows, value_width), BF16),
            struct((rows + key_rows, LANES), BF16),
        ),
        in_specs=[SMEM, SMEM, VMEM, VMEM, HBM],
        out_specs=(SMEM, HBM, HBM),
        scratch_shapes=[
            pltpu.VMEM((2, key_rows, LANES), BF16),
            pltpu.VMEM((8, LANES), F32),
            pltpu.SemaphoreType.DMA((2, W * frames + 4)),
        ],
        compiler_params=params(16),
        name="lists_and_edges",
    )(block_list, block_count, memory_key, shrinkage, memory_value)
    more_edges = pl.pallas_call(
        functools.partial(edge_chunks, sizes, n_chunks),
        out_shape=[struct((rows, LANES), BF16)] * (n_chunks - 1),
        in_specs=[HBM],
        out_specs=[HBM] * (n_chunks - 1),
        scratch_shapes=[pltpu.SemaphoreType.DMA((n_chunks - 1, W * frames))],
        compiler_params=params(16),
        name="edge_chunks",
    )(memory_value)

    on_chip = [(i ^ 1, i) for i in range(n_space)]
    over_link = []
    for i in range(1, n_space - 1, 2):
        over_link += [(i, i + 1), (i + 1, i)]
    link_halo = [lax.ppermute(link_edge, "space", over_link)]
    chip_halo = lax.ppermute(chip_edge, "space", on_chip)
    for edge in more_edges:
        link_halo.append(lax.ppermute(edge, "space", over_link))

    acc, own_top, own_total, cat, self_term = pl.pallas_call(
        functools.partial(own_part, sizes),
        out_shape=(
            struct((n_blocks + 1, BS, value_width), F32),
            struct((n_blocks + 1, BS, LANES), F32),
            struct((n_blocks + 1, BS, LANES), F32),
            struct((n_blocks + 1, BS, 2 * key_width), BF16),
            struct((n_blocks + 1, BS, LANES), F32),
        ),
        in_specs=[SMEM, VMEM, VMEM, VMEM, VMEM, HBM],
        out_specs=(VMEM,) * 5,
        scratch_shapes=[
            pltpu.VMEM((n_blocks, frames * BS, 2 * key_width), BF16),
            pltpu.VMEM((n_blocks, 1, frames * BS), F32),
            pltpu.VMEM((max_own, BS, frames * BS), F32),
            pltpu.VMEM(memory_value.shape, BF16),
            pltpu.SemaphoreType.DMA,
        ],
        compiler_params=params(44),
        name="own_part",
    )(pairs, query, select, memory_key, shrinkage, memory_value)

    weights, factor, stats = pl.pallas_call(
        functools.partial(halo_scores, sizes),
        out_shape=(
            struct((max_halo, BS, frames * BS), BF16),
            struct((n_blocks + 1, BS, LANES), F32),
            struct((2 * n_blocks, LANES), F32),
        ),
        grid=(1,),
        in_specs=[
            SMEM,
            VMEM,
            VMEM,
            pl.BlockSpec((chip_key_rows, value_width), lambda i: (rows // chip_key_rows, 0))
            if rows % chip_key_rows == 0
            else pl.BlockSpec((pl.Element(chip_key_rows), pl.Element(value_width)), lambda i: (rows, 0)),
            pl.BlockSpec((pl.Element(key_rows), pl.Element(LANES)), lambda i: (rows, 0)),
            VMEM,
            VMEM,
        ],
        out_specs=(HBM, VMEM, VMEM),
        scratch_shapes=[
            pltpu.VMEM((2 * W, frames * BS, 2 * key_width), BF16),
            pltpu.VMEM((2 * W, 1, frames * BS), F32),
            pltpu.VMEM((max_halo, BS, frames * BS), F32),
            pltpu.VMEM((n_blocks + 1, BS, LANES), F32),
            pltpu.VMEM((n_blocks + 1, BS, LANES), F32),
            pltpu.VMEM((max_halo, BS, frames * BS), BF16),
            pltpu.SemaphoreType.DMA((max_halo,)),
        ],
        compiler_params=params(44),
        name="halo_scores",
    )(pairs, cat, self_term, chip_halo, link_halo[0], own_top, own_total)

    mine, other = [], []
    swap = [(i ^ 1, i) for i in range(n_tm)]
    for c in range(n_chunks):
        out_rows = pixels + (6 * n_blocks if c == 0 else 0)
        x = pl.pallas_call(
            functools.partial(chunk_sums, sizes, c),
            out_shape=struct((out_rows, LANES), BF16),
            grid=(1,),
            in_specs=[
                SMEM,
                HBM,
                pl.BlockSpec((n_blocks, BS, LANES), lambda i, c=c: (0, 0, c)),
                VMEM,
                VMEM,
                pl.BlockSpec((rows, LANES), lambda i, c=c: (0, c)),
                pl.BlockSpec((rows, LANES), lambda i: (0, 0)),
            ],
            out_specs=pl.BlockSpec((out_rows, LANES), lambda i: (0, 0)),
            scratch_shapes=[
                pltpu.VMEM((max_halo, BS, frames * BS), BF16),
                pltpu.VMEM((n_blocks + 1, BS, LANES), F32),
                pltpu.SemaphoreType.DMA((max_halo,)),
            ],
            compiler_params=params(32),
            name=f"chunk_sums_{c}",
        )(pairs, weights, acc, factor, stats, chip_halo, link_halo[c])
        mine.append(x)
        other.append(lax.ppermute(x, "tm", swap) if n_tm == 2 else lax.all_gather(x, "tm"))

    if n_tm == 2:
        out = pl.pallas_call(
            functools.partial(combine, sizes, n_chunks),
            out_shape=struct((pixels, value_width), BF16),
            in_specs=[VMEM] * (2 * n_chunks),
            out_specs=VMEM,
            compiler_params=params(32),
            name="combine",
        )(*mine, *other)
    else:
        packed = other[0][:, pixels:, :]
        tops, totals = zip(*[unpack_stats(packed[i], n_blocks) for i in range(n_tm)])
        tops = jnp.stack(tops).reshape(n_tm, pixels, 1)
        totals = jnp.stack(totals).reshape(n_tm, pixels, 1)
        factors = jnp.exp2(tops - jnp.max(tops, axis=0, keepdims=True))
        total = jnp.sum(totals * factors, axis=0)
        sums = [jnp.sum(x[:, :pixels, :].astype(F32) * factors, axis=0) / total for x in other]
        out = jnp.concatenate(sums, axis=1).astype(BF16)
    return out[None]


def solution(mesh):
    in_specs = (
        P(None, "space", None),
        P(None, "space", None),
        P("tm", "space", None),
        P("tm", "space"),
        P("tm", "space", None),
        P("space", None),
        P("space"),
    )
    out_specs = P(None, "space", None)
    body = functools.partial(shards, mesh.shape["space"], mesh.shape["tm"])
    return jax.shard_map(body, mesh=mesh, in_specs=in_specs, out_specs=out_specs, check_vma=False)
```

```python
import functools
import math

import jax
import jax.numpy as jnp
from jax import lax
from jax.experimental import pallas as pl
from jax.experimental.pallas import tpu as pltpu
from jax.sharding import PartitionSpec as P

BS = 128
W = 2
LANES = 128
EDGE = W * BS
NONE = -1e30
OWN_AT, HALO_AT, COUNT_AT = 0, 64, 128
F32, BF16 = jnp.float32, jnp.bfloat16

VMEM = pl.BlockSpec(memory_space=pltpu.VMEM)
SMEM = pl.BlockSpec(memory_space=pltpu.SMEM)
HBM = pl.BlockSpec(memory_space=pltpu.HBM)


def params(mib):
    return pltpu.CompilerParams(vmem_limit_bytes=mib * 1024 * 1024)


def row_to_lanes(row):
    return jnp.transpose(jnp.broadcast_to(row, (row.shape[1], row.shape[1])))


def lane_tiles(x):
    return [x[:, i * LANES : (i + 1) * LANES] for i in range(x.shape[1] // LANES)]


def wide(x, times):
    return jnp.concatenate([x] * times, axis=1)


def run_all(copies):
    for copy in copies:
        copy.start()
    for copy in copies:
        copy.wait()


def value_copies(sizes, value_ref, out, start, lanes, sems):
    frames = sizes[0]
    return [
        pltpu.make_async_copy(
            value_ref.at[f, pl.ds(start + e * BS, BS), lanes],
            out.at[pl.ds((e * frames + f) * BS, BS), :],
            sems.at[e * frames + f],
        )
        for e in range(W)
        for f in range(frames)
    ]


def edge_start(pixels, over_link):
    odd = lax.rem(lax.axis_index("space"), 2)
    side = odd if over_link else 1 - odd
    return pl.multiple_of(side * (pixels - EDGE), EDGE)


def shrink_rows(sizes, shrink, start):
    frames = sizes[0]
    edge = shrink[:, pl.ds(start, EDGE)].astype(F32)
    rows = [edge[:, e * BS : (e + 1) * BS] for e in range(W)]
    pad = jnp.zeros((16 - W * frames, LANES), F32)
    return jnp.concatenate(rows + [pad], axis=0).astype(BF16)


def lists_and_edge(
    sizes, list_ref, count_ref, key_ref, shrink_ref, value_ref, pairs_ref, link_ref,
    list_sc, count_sc, shrink_sc, sems, key_sems, small_sems,
):
    frames, pixels, n_blocks, n_listed, key_width, value_width = sizes
    start = edge_start(pixels, True)
    small = [
        pltpu.make_async_copy(list_ref, list_sc, small_sems.at[0]),
        pltpu.make_async_copy(count_ref, count_sc, small_sems.at[1]),
        pltpu.make_async_copy(shrink_ref, shrink_sc, small_sems.at[2]),
    ]
    for copy in small:
        copy.start()
    copies = value_copies(sizes, value_ref, link_ref, start, pl.ds(0, LANES), sems)
    at = frames * EDGE
    for e in range(W):
        for f in range(frames):
            copies.append(
                pltpu.make_async_copy(
                    key_ref.at[f, :, pl.ds(start + e * BS, BS)],
                    link_ref.at[pl.ds(at, key_width), :],
                    key_sems.at[e * frames + f],
                )
            )
            at += key_width
    for copy in copies:
        copy.start()
    for copy in small:
        copy.wait()
    link_ref[at : at + 16, :] = shrink_rows(sizes, shrink_sc, start)
    odd = lax.rem(lax.axis_index("space"), 2)

    def block(b, carry):
        live = count_sc[b]
        for j in range(n_listed):
            n_own, n_halo = carry
            l = list_sc[b, j]
            ok = j < live
            inside = (l >= W) & (l < W + n_blocks)
            right = jnp.where(l >= W + n_blocks, 1, 0)
            e = jnp.where(right == 1, l - (W + n_blocks), l)
            over_link = jnp.where(right == odd, 1, 0)
            pairs_ref[OWN_AT + n_own] = b * n_blocks + jnp.clip(l - W, 0, n_blocks - 1)
            pairs_ref[HALO_AT + n_halo] = b * 4 + over_link * W + jnp.clip(e, 0, W - 1)
            carry = (
                n_own + jnp.where(ok & inside, 1, 0),
                n_halo + jnp.where(ok & jnp.logical_not(inside), 1, 0),
            )
        return carry

    n_own, n_halo = lax.fori_loop(0, n_blocks, block, (0, 0))
    pairs_ref[OWN_AT + n_own] = n_blocks * n_blocks
    pairs_ref[HALO_AT + n_halo] = n_blocks * 4
    pairs_ref[COUNT_AT] = n_own
    pairs_ref[COUNT_AT + 1] = n_halo
    for copy in copies:
        copy.wait()


def chip_edge_and_chunk(
    sizes, query_ref, select_ref, key_ref, shrink_ref, value_ref, after_ref,
    chip_ref, link_ref, query_out, select_out, key_out, shrink_out,
    sems, key_sems, small_sems,
):
    frames, pixels, n_blocks, n_listed, key_width, value_width = sizes
    start = edge_start(pixels, False)
    small = pltpu.make_async_copy(shrink_ref, shrink_out, small_sems.at[0])
    small.start()
    copies = value_copies(sizes, value_ref, chip_ref, start, slice(None), sems.at[0])
    at = frames * EDGE
    for e in range(W):
        for f in range(frames):
            copies.append(
                pltpu.make_async_copy(
                    key_ref.at[f, :, pl.ds(start + e * BS, BS)],
                    chip_ref.at[pl.ds(at, key_width), pl.ds(f * BS, BS)],
                    key_sems.at[e * frames + f],
                )
            )
        at += key_width
    copies += value_copies(sizes, value_ref, link_ref, edge_start(pixels, True), pl.ds(LANES, LANES), sems.at[1])
    copies += [
        pltpu.make_async_copy(query_ref, query_out, small_sems.at[1]),
        pltpu.make_async_copy(select_ref, select_out, small_sems.at[2]),
        pltpu.make_async_copy(key_ref, key_out, small_sems.at[3]),
    ]
    for copy in copies:
        copy.start()
    small.wait()
    chip_ref[at : at + 16, :LANES] = shrink_rows(sizes, shrink_out, start)
    for copy in copies:
        copy.wait()


def link_chunks(sizes, first, value_ref, after_ref, *refs):
    outs, sems = refs[:-1], refs[-1]
    start = edge_start(sizes[1], True)
    copies = []
    for i, out in enumerate(outs):
        copies += value_copies(sizes, value_ref, out, start, pl.ds((first + i) * LANES, LANES), sems.at[i])
    run_all(copies)


def paired(count, body):
    def step(i, carry):
        body(2 * i)
        body(2 * i + 1)
        return carry

    lax.fori_loop(0, (count + 1) // 2, step, 0)


def squares_over(k):
    k_f = k.astype(F32)
    return jnp.concatenate([(k_f * k_f).astype(BF16), k], axis=0)


def own_part(
    sizes, pairs_ref, query_ref, select_ref, key_ref, shrink_ref, value_ref,
    weight_ref, rest_ref, acc_ref, top_ref, total_ref, cat_ref, self_ref,
    keys_sc, shr_sc, score_sc, value_sc, sems,
):
    frames, pixels, n_blocks, n_listed, key_width, value_width = sizes
    cols = frames * BS
    half = value_width // 2
    bits = int(math.log2(n_blocks))
    values = [
        pltpu.make_async_copy(value_ref.at[:, :, pl.ds(0, half)], value_sc, sems.at[0]),
        pltpu.make_async_copy(value_ref.at[:, :, pl.ds(half, half)], rest_ref, sems.at[1]),
    ]
    for copy in values:
        copy.start()
    scale = -math.log2(math.e) / math.sqrt(key_width)
    for b in range(n_blocks):
        block = slice(b * BS, (b + 1) * BS)
        q = query_ref[:, block].astype(F32)
        s = select_ref[:, block].astype(F32)
        both = jnp.concatenate([s, -2.0 * q * s], axis=0)
        cat_ref[b] = jnp.transpose(both).astype(BF16)
        self_ref[b] = row_to_lanes(jnp.sum(s * q * q, axis=0, keepdims=True))
    cat_ref[n_blocks] = jnp.zeros((BS, 2 * key_width), BF16)
    self_ref[n_blocks] = jnp.zeros((BS, LANES), F32)
    shrink = shrink_ref[...].astype(F32) * scale
    for l in range(n_blocks):
        for f in range(frames):
            block = slice(l * BS, (l + 1) * BS)
            keys_sc[l, :, f * BS : (f + 1) * BS] = squares_over(key_ref[f, :, block])
            shr_sc[l, :, f * BS : (f + 1) * BS] = shrink[f : f + 1, block]
    top_ref[...] = jnp.full_like(top_ref, NONE)
    total_ref[...] = jnp.zeros_like(total_ref)
    acc_ref[...] = jnp.zeros_like(acc_ref)
    count = pairs_ref[COUNT_AT]

    def score(p):
        code = pairs_ref[OWN_AT + p]
        b, l = code >> bits, code & (n_blocks - 1)
        s = jnp.dot(cat_ref[b], keys_sc[l], preferred_element_type=F32)
        s = (s + wide(self_ref[b], frames)) * shr_sc[l]
        score_sc[p] = s
        top_ref[b] = functools.reduce(jnp.maximum, lane_tiles(s), top_ref[b])

    paired(count, score)
    for b in range(n_blocks):
        top_ref[b] = jnp.broadcast_to(jnp.max(top_ref[b], axis=1, keepdims=True), (BS, LANES))
    values[0].wait()

    def read(p):
        code = pairs_ref[OWN_AT + p]
        b, l = code >> bits, code & (n_blocks - 1)
        w = jnp.exp2(score_sc[p] - wide(top_ref[b], frames))
        total_ref[b] = functools.reduce(jnp.add, lane_tiles(w), total_ref[b])
        w = w.astype(BF16)
        weight_ref[p] = w
        v = value_sc[:, pl.ds(pl.multiple_of(l * BS, BS), BS), :].reshape(cols, half)
        acc_ref[b] += jnp.dot(w, v, preferred_element_type=F32)

    paired(count, read)
    values[1].wait()


def own_rest(sizes, pairs_ref, weight_ref, value_ref, after_ref, acc_ref):
    frames, pixels, n_blocks = sizes[:3]
    bits = int(math.log2(n_blocks))
    acc_ref[...] = jnp.zeros_like(acc_ref)

    def read(p):
        code = pairs_ref[OWN_AT + p]
        b, l = code >> bits, code & (n_blocks - 1)
        v = value_ref[:, pl.ds(pl.multiple_of(l * BS, BS), BS), :].reshape(frames * BS, value_ref.shape[2])
        acc_ref[b] += jnp.dot(weight_ref[p], v, preferred_element_type=F32)

    paired(pairs_ref[COUNT_AT], read)


def halo_scores(
    sizes, pairs_ref, cat_ref, self_ref, chip_ref, link_ref, own_top_ref, own_total_ref,
    weight_ref, factor_ref, stats_ref,
    keys_sc, shr_sc, score_sc, top_sc, total_sc,
):
    frames, pixels, n_blocks, n_listed, key_width, value_width = sizes
    rows = frames * EDGE
    scale = -math.log2(math.e) / math.sqrt(key_width)
    for e in range(W):
        at = rows + e * key_width
        keys_sc[e] = squares_over(chip_ref[at : at + key_width, :])
        for f in range(frames):
            at = rows + (e * frames + f) * key_width
            keys_sc[W + e, :, f * BS : (f + 1) * BS] = squares_over(link_ref[at : at + key_width, :])
    shrinks = [
        chip_ref[rows + W * key_width :, :LANES].astype(F32) * scale,
        link_ref[rows + W * frames * key_width :, :].astype(F32) * scale,
    ]
    for side in range(2):
        for e in range(W):
            for f in range(frames):
                at = e * frames + f
                shr_sc[side * W + e, :, f * BS : (f + 1) * BS] = shrinks[side][at : at + 1, :]
    top_sc[...] = jnp.full_like(top_sc, NONE)
    total_sc[...] = jnp.zeros_like(total_sc)
    count = pairs_ref[COUNT_AT + 1]

    def score(p):
        code = pairs_ref[HALO_AT + p]
        b, h = code >> 2, code & 3
        s = jnp.dot(cat_ref[b], keys_sc[h], preferred_element_type=F32)
        s = (s + wide(self_ref[b], frames)) * shr_sc[h]
        score_sc[p] = s
        top_sc[b] = functools.reduce(jnp.maximum, lane_tiles(s), top_sc[b])

    paired(count, score)
    for b in range(n_blocks):
        own = own_top_ref[b]
        top = jnp.maximum(own, jnp.broadcast_to(jnp.max(top_sc[b], axis=1, keepdims=True), (BS, LANES)))
        top_sc[b] = top
        factor_ref[b] = jnp.exp2(own - top)

    def weigh(p):
        code = pairs_ref[HALO_AT + p]
        b = code >> 2
        w = jnp.exp2(score_sc[p] - wide(top_sc[b], frames))
        total_sc[b] = functools.reduce(jnp.add, lane_tiles(w), total_sc[b])
        weight_ref[p] = w.astype(BF16)

    paired(count, weigh)
    for b in range(n_blocks):
        total = jnp.sum(total_sc[b] + own_total_ref[b] * factor_ref[b], axis=1, keepdims=True)
        stats_ref[b : b + 1, :] = jnp.transpose(top_sc[b])[:1, :]
        stats_ref[n_blocks + b : n_blocks + b + 1, :] = jnp.transpose(jnp.broadcast_to(total, (BS, LANES)))[:1, :]


def chunk_sums(sizes, c, pairs_ref, weight_ref, acc_ref, factor_ref, stats_ref, chip_ref, link_ref, out_ref, sum_sc):
    frames, pixels, n_blocks, n_listed, key_width, value_width = sizes
    cols = frames * BS
    per_half = acc_ref.shape[2] // LANES
    half_lanes = slice((c % per_half) * LANES, (c % per_half + 1) * LANES)
    for b in range(n_blocks):
        sum_sc[b] = acc_ref[b, :, half_lanes] * factor_ref[b]
    sum_sc[n_blocks] = jnp.zeros((BS, LANES), F32)

    def add(p):
        code = pairs_ref[HALO_AT + p]
        b, h = code >> 2, code & 3
        at = pl.multiple_of((h & (W - 1)) * cols, cols)
        chip = chip_ref[pl.ds(at, cols), c * LANES : (c + 1) * LANES]
        v = jnp.where(h >= W, link_ref[pl.ds(at, cols), :], chip)
        sum_sc[b] += jnp.dot(weight_ref[p], v, preferred_element_type=F32)

    paired(pairs_ref[COUNT_AT + 1], add)
    for b in range(n_blocks):
        out_ref[b * BS : (b + 1) * BS, :] = sum_sc[b].astype(BF16)
    if c == 0:
        rest = stats_ref[...]
        for i in range(3):
            piece = rest.astype(BF16)
            rest = rest - piece.astype(F32)
            out_ref[pixels + i * 2 * n_blocks : pixels + (i + 1) * 2 * n_blocks, :] = piece


def unpack_stats(x, n_blocks):
    n = 2 * n_blocks
    x = x.astype(F32)
    x = (x[:n] + x[n : 2 * n]) + x[2 * n :]
    return x[:n_blocks], x[n_blocks:]


def combine(sizes, n_chunks, *refs):
    frames, pixels, n_blocks = sizes[:3]
    mine, other, out_ref = refs[:n_chunks], refs[n_chunks : 2 * n_chunks], refs[-1]

    def run(first, second):
        top_a, total_a = unpack_stats(first[0][pixels:, :], n_blocks)
        top_b, total_b = unpack_stats(second[0][pixels:, :], n_blocks)
        top = jnp.maximum(top_a, top_b)
        a, b = jnp.exp2(top_a - top), jnp.exp2(top_b - top)
        total = total_a * a + total_b * b
        a, b = a / total, b / total
        for i in range(n_blocks):
            col_a = row_to_lanes(a[i : i + 1, :])
            col_b = row_to_lanes(b[i : i + 1, :])
            r = slice(i * BS, (i + 1) * BS)
            for c in range(n_chunks):
                x = first[c][r, :].astype(F32) * col_a + second[c][r, :].astype(F32) * col_b
                out_ref[r, c * LANES : (c + 1) * LANES] = x.astype(BF16)

    me = lax.axis_index("tm")

    @pl.when(me == 0)
    def _():
        run(mine, other)

    @pl.when(me != 0)
    def _():
        run(other, mine)


def shards(n_space, n_tm, query_key, selection, memory_key, shrinkage, memory_value, block_list, block_count):
    frames, pixels, key_width = memory_key.shape
    value_width = memory_value.shape[2]
    n_blocks, n_listed = block_list.shape
    sizes = (frames, pixels, n_blocks, n_listed, key_width, value_width)
    n_chunks = value_width // LANES
    half = value_width // 2
    cols = frames * BS
    rows = frames * EDGE
    link_rows = rows + W * frames * key_width + 16
    chip_rows = rows + W * key_width + 16
    max_halo = n_blocks * min(n_listed, 2 * W) + 2
    max_own = n_blocks * n_listed + 2
    struct = jax.ShapeDtypeStruct
    dma = pltpu.SemaphoreType.DMA
    query, select = jnp.swapaxes(query_key[0], 0, 1), jnp.swapaxes(selection[0], 0, 1)
    keys = jnp.swapaxes(memory_key, 1, 2)
    query, select, keys, shrinkage, memory_value, block_list, block_count = [
        pltpu.with_memory_space_constraint(x, pltpu.HBM)
        for x in (query, select, keys, shrinkage, memory_value, block_list, block_count)
    ]
    on_chip = [(i ^ 1, i) for i in range(n_space)]
    over_link = []
    for i in range(1, n_space - 1, 2):
        over_link += [(i, i + 1), (i + 1, i)]
    swap = [(i ^ 1, i) for i in range(n_tm)]

    pairs, link_edge = pl.pallas_call(
        functools.partial(lists_and_edge, sizes),
        out_shape=(struct((256,), jnp.int32), struct((link_rows, LANES), BF16)),
        in_specs=[HBM] * 5,
        out_specs=(SMEM, VMEM),
        scratch_shapes=[
            pltpu.SMEM(block_list.shape, jnp.int32),
            pltpu.SMEM(block_count.shape, jnp.int32),
            pltpu.VMEM(shrinkage.shape, BF16),
            dma((W * frames,)),
            dma((W * frames,)),
            dma((3,)),
        ],
        compiler_params=params(1),
        name="lists_and_edge",
    )(block_list, block_count, keys, shrinkage, memory_value)
    link_halo = [lax.ppermute(link_edge, "space", over_link)]
    chip_edge, link_edge, query, select, near_keys, near_shrink = pl.pallas_call(
        functools.partial(chip_edge_and_chunk, sizes),
        out_shape=(
            struct((chip_rows, value_width), BF16),
            struct((rows, LANES), BF16),
            struct(query.shape, BF16),
            struct(select.shape, BF16),
            struct(keys.shape, BF16),
            struct(shrinkage.shape, BF16),
        ),
        in_specs=[HBM] * 5 + [VMEM],
        out_specs=(VMEM,) * 6,
        scratch_shapes=[dma((2, W * frames)), dma((W * frames,)), dma((4,))],
        compiler_params=params(1),
        name="chip_edge_and_chunk",
    )(query, select, keys, shrinkage, memory_value, link_edge)
    chip_halo = lax.ppermute(chip_edge, "space", on_chip)
    link_halo.append(lax.ppermute(link_edge, "space", over_link))

    own_weights, rest, acc, own_top, own_total, cat, self_term = pl.pallas_call(
        functools.partial(own_part, sizes),
        out_shape=(
            struct((max_own, BS, cols), BF16),
            struct((frames, pixels, value_width - half), BF16),
            struct((n_blocks + 1, BS, half), F32),
            struct((n_blocks + 1, BS, LANES), F32),
            struct((n_blocks + 1, BS, LANES), F32),
            struct((n_blocks + 1, BS, 2 * key_width), BF16),
            struct((n_blocks + 1, BS, LANES), F32),
        ),
        in_specs=[SMEM, VMEM, VMEM, VMEM, VMEM, HBM],
        out_specs=(VMEM,) * 7,
        scratch_shapes=[
            pltpu.VMEM((n_blocks, 2 * key_width, cols), BF16),
            pltpu.VMEM((n_blocks, 1, cols), F32),
            pltpu.VMEM((max_own, BS, cols), F32),
            pltpu.VMEM((frames, pixels, half), BF16),
            dma((2,)),
        ],
        compiler_params=params(20),
        name="own_part",
    )(pairs, query, select, near_keys, near_shrink, memory_value)

    more_edges = pl.pallas_call(
        functools.partial(link_chunks, sizes, 2),
        out_shape=[struct((rows, LANES), BF16)] * (n_chunks - 2),
        in_specs=[HBM, VMEM],
        out_specs=[VMEM] * (n_chunks - 2),
        scratch_shapes=[dma((n_chunks - 2, W * frames))],
        compiler_params=params(1),
        name="link_chunks",
    )(memory_value, own_top)
    for edge in more_edges:
        link_halo.append(lax.ppermute(edge, "space", over_link))

    weights, factor, stats = pl.pallas_call(
        functools.partial(halo_scores, sizes),
        out_shape=(
            struct((max_halo, BS, cols), BF16),
            struct((n_blocks + 1, BS, LANES), F32),
            struct((2 * n_blocks, LANES), F32),
        ),
        in_specs=[SMEM] + [VMEM] * 6,
        out_specs=(VMEM,) * 3,
        scratch_shapes=[
            pltpu.VMEM((2 * W, 2 * key_width, cols), BF16),
            pltpu.VMEM((2 * W, 1, cols), F32),
            pltpu.VMEM((max_halo, BS, cols), F32),
            pltpu.VMEM((n_blocks + 1, BS, LANES), F32),
            pltpu.VMEM((n_blocks + 1, BS, LANES), F32),
        ],
        compiler_params=params(12),
        name="halo_scores",
    )(pairs, cat, self_term, chip_halo, link_halo[0], own_top, own_total)

    mine, other = [], []
    for c in range(n_chunks):
        if c * LANES == half:
            acc = pl.pallas_call(
                functools.partial(own_rest, sizes),
                out_shape=struct((n_blocks + 1, BS, value_width - half), F32),
                in_specs=[SMEM] + [VMEM] * 3,
                out_specs=VMEM,
                compiler_params=params(2),
                name="own_rest",
            )(pairs, own_weights, rest, mine[0])
        out_rows = pixels + (6 * n_blocks if c == 0 else 0)
        x = pl.pallas_call(
            functools.partial(chunk_sums, sizes, c),
            out_shape=struct((out_rows, LANES), BF16),
            in_specs=[SMEM] + [VMEM] * 6,
            out_specs=VMEM,
            scratch_shapes=[pltpu.VMEM((n_blocks + 1, BS, LANES), F32)],
            compiler_params=params(2),
            name=f"chunk_sums_{c}",
        )(pairs, weights, acc, factor, stats, chip_halo, link_halo[c])
        mine.append(x)
        other.append(lax.ppermute(x, "tm", swap) if n_tm == 2 else lax.all_gather(x, "tm"))

    if n_tm == 2:
        out = pl.pallas_call(
            functools.partial(combine, sizes, n_chunks),
            out_shape=struct((pixels, value_width), BF16),
            in_specs=[VMEM] * (2 * n_chunks),
            out_specs=VMEM,
            compiler_params=params(2),
            name="combine",
        )(*mine, *other)
    else:
        packed = other[0][:, pixels:, :]
        tops, totals = zip(*[unpack_stats(packed[i], n_blocks) for i in range(n_tm)])
        tops = jnp.stack(tops).reshape(n_tm, pixels, 1)
        totals = jnp.stack(totals).reshape(n_tm, pixels, 1)
        factors = jnp.exp2(tops - jnp.max(tops, axis=0, keepdims=True))
        total = jnp.sum(totals * factors, axis=0)
        sums = [jnp.sum(x[:, :pixels, :].astype(F32) * factors, axis=0) / total for x in other]
        out = jnp.concatenate(sums, axis=1).astype(BF16)
    return out[None]


def solution(mesh):
    in_specs = (
        P(None, "space", None),
        P(None, "space", None),
        P("tm", "space", None),
        P("tm", "space"),
        P("tm", "space", None),
        P("space", None),
        P("space"),
    )
    out_specs = P(None, "space", None)
    body = functools.partial(shards, mesh.shape["space"], mesh.shape["tm"])
    return jax.shard_map(body, mesh=mesh, in_specs=in_specs, out_specs=out_specs, check_vma=False)
```

```python
import functools
import math

import jax
import jax.numpy as jnp
from jax import lax
from jax.experimental import pallas as pl
from jax.experimental.pallas import tpu as pltpu
from jax.sharding import PartitionSpec as P

BS = 128
W = 2
LANES = 128
EDGE = W * BS
NONE = -1e30
WIDTH = 128
UNROLL = 4
OWN_AT, HALO_AT, COUNT_AT = 0, 64, 128
F32, BF16 = jnp.float32, jnp.bfloat16

VMEM = pl.BlockSpec(memory_space=pltpu.VMEM)
SMEM = pl.BlockSpec(memory_space=pltpu.SMEM)
HBM = pl.BlockSpec(memory_space=pltpu.HBM)


def params(mib):
    return pltpu.CompilerParams(vmem_limit_bytes=mib * 1024 * 1024)


def row_to_lanes(row):
    return jnp.transpose(jnp.broadcast_to(row, (row.shape[1], row.shape[1])))


def lane_tiles(x):
    return [x[:, i * LANES : (i + 1) * LANES] for i in range(x.shape[1] // LANES)]


def wide(x, times):
    return jnp.concatenate([x] * times, axis=1)


def value_copies(sizes, value_ref, out, start, lanes, sems):
    frames = sizes[0]
    return [
        pltpu.make_async_copy(
            value_ref.at[f, pl.ds(start + e * BS, BS), lanes],
            out.at[pl.ds((e * frames + f) * BS, BS), :],
            sems.at[e * frames + f],
        )
        for e in range(W)
        for f in range(frames)
    ]


def key_place(sizes, e, f):
    frames, key_width = sizes[0], sizes[4]
    per_row = WIDTH // LANES
    i = e * frames + f
    at, lane = frames * EDGE + i // per_row * key_width, i % per_row * LANES
    return slice(at, at + key_width), slice(lane, lane + LANES)


def edge_start(pixels, over_link):
    odd = lax.rem(lax.axis_index("space"), 2)
    side = odd if over_link else 1 - odd
    return pl.multiple_of(side * (pixels - EDGE), EDGE)


def shrink_rows(sizes, shrink, start):
    frames = sizes[0]
    edge = shrink[:, pl.ds(start, EDGE)].astype(F32)
    rows = [edge[:, e * BS : (e + 1) * BS] for e in range(W)]
    pad = jnp.zeros((16 - W * frames, LANES), F32)
    return jnp.concatenate(rows + [pad], axis=0).astype(BF16)


def lists_and_edge(
    sizes, list_ref, count_ref, query_ref, select_ref, key_ref, shrink_ref, value_ref,
    pairs_ref, link_ref, chip_ref, query_out, select_out, key_out, shrink_out,
    list_sc, count_sc, sems, key_sems, small_sems,
):
    frames, pixels, n_blocks, n_listed, key_width, value_width = sizes
    start = edge_start(pixels, True)
    small = [
        pltpu.make_async_copy(list_ref, list_sc, small_sems.at[0]),
        pltpu.make_async_copy(count_ref, count_sc, small_sems.at[1]),
        pltpu.make_async_copy(shrink_ref, shrink_out, small_sems.at[2]),
    ]
    for copy in small:
        copy.start()
    copies = value_copies(sizes, value_ref, link_ref, start, pl.ds(0, WIDTH), sems.at[0])
    for e in range(W):
        for f in range(frames):
            copies.append(
                pltpu.make_async_copy(
                    key_ref.at[f, :, pl.ds(start + e * BS, BS)],
                    link_ref.at[key_place(sizes, e, f)],
                    key_sems.at[e * frames + f],
                )
            )
    copies += [
        pltpu.make_async_copy(query_ref, query_out, small_sems.at[3]),
        pltpu.make_async_copy(select_ref, select_out, small_sems.at[4]),
        pltpu.make_async_copy(key_ref, key_out, small_sems.at[5]),
    ]
    chip_start = edge_start(pixels, False)
    copies += value_copies(sizes, value_ref, chip_ref, chip_start, slice(None), sems.at[1])
    chip_at = frames * EDGE
    for e in range(W):
        for f in range(frames):
            copies.append(
                pltpu.make_async_copy(
                    key_ref.at[f, :, pl.ds(chip_start + e * BS, BS)],
                    chip_ref.at[pl.ds(chip_at, key_width), pl.ds(f * BS, BS)],
                    key_sems.at[(W + e) * frames + f],
                )
            )
        chip_at += key_width
    for copy in copies:
        copy.start()
    for copy in small:
        copy.wait()
    link_ref[link_ref.shape[0] - 16 :, :LANES] = shrink_rows(sizes, shrink_out, start)
    chip_ref[chip_at : chip_at + 16, :LANES] = shrink_rows(sizes, shrink_out, chip_start)
    odd = lax.rem(lax.axis_index("space"), 2)

    left, right = W * (1 - odd), W * odd - (W + n_blocks)

    def block(b, carry):
        n_own, n_halo = carry
        live = count_sc[b]
        for j in range(n_listed):
            l = list_sc[b, j]
            inside = (l >= W) & (l < W + n_blocks)
            pairs_ref[OWN_AT + n_own] = b * n_blocks + (l - W)
            pairs_ref[HALO_AT + n_halo] = b * 4 + l + jnp.where(l >= W, right, left)
            n_own += jnp.where((j < live) & inside, 1, 0)
            n_halo += jnp.where((j < live) & jnp.logical_not(inside), 1, 0)
        return n_own, n_halo

    n_own, n_halo = lax.fori_loop(0, n_blocks, block, (0, 0))
    for i in range(UNROLL - 1):
        pairs_ref[OWN_AT + n_own + i] = n_blocks * n_blocks
        pairs_ref[HALO_AT + n_halo + i] = n_blocks * 4
    pairs_ref[COUNT_AT] = n_own
    pairs_ref[COUNT_AT + 1] = n_halo
    for copy in copies:
        copy.wait()


def unrolled(count, body):
    def step(i, carry):
        for k in range(UNROLL):
            body(UNROLL * i + k)
        return carry

    lax.fori_loop(0, (count + UNROLL - 1) // UNROLL, step, 0)


def squares_over(k):
    k_f = k.astype(F32)
    return jnp.concatenate([(k_f * k_f).astype(BF16), k], axis=0)


def own_part(
    sizes, pairs_ref, query_ref, select_ref, key_ref, shrink_ref, value_ref,
    acc_ref, top_ref, total_ref, cat_ref, self_ref, *refs,
):
    links, (keys_sc, shr_sc, score_sc, value_sc, sem, edge_sems) = refs[:-6], refs[-6:]
    frames, pixels, n_blocks, n_listed, key_width, value_width = sizes
    cols = frames * BS
    bits = int(math.log2(n_blocks))
    values = pltpu.make_async_copy(value_ref, value_sc, sem)
    values.start()
    edges = []
    for i, link in enumerate(links):
        lanes = pl.ds((i + 1) * WIDTH, WIDTH)
        edges += value_copies(sizes, value_ref, link, edge_start(pixels, True), lanes, edge_sems.at[i])
    for copy in edges:
        copy.start()
    scale = -math.log2(math.e) / math.sqrt(key_width)
    for b in range(n_blocks):
        block = slice(b * BS, (b + 1) * BS)
        q = query_ref[:, block].astype(F32)
        s = select_ref[:, block].astype(F32)
        both = jnp.concatenate([s, -2.0 * q * s], axis=0)
        cat_ref[b] = jnp.transpose(both).astype(BF16)
        self_ref[b] = row_to_lanes(jnp.sum(s * q * q, axis=0, keepdims=True))
    cat_ref[n_blocks] = jnp.zeros((BS, 2 * key_width), BF16)
    self_ref[n_blocks] = jnp.zeros((BS, LANES), F32)
    shrink = shrink_ref[...].astype(F32) * scale
    for l in range(n_blocks):
        for f in range(frames):
            block = slice(l * BS, (l + 1) * BS)
            keys_sc[l, :, f * BS : (f + 1) * BS] = squares_over(key_ref[f, :, block])
            shr_sc[l, :, f * BS : (f + 1) * BS] = shrink[f : f + 1, block]
    top_ref[...] = jnp.full_like(top_ref, NONE)
    total_ref[...] = jnp.zeros_like(total_ref)
    acc_ref[...] = jnp.zeros_like(acc_ref)
    count = pairs_ref[COUNT_AT]

    def score(p):
        code = pairs_ref[OWN_AT + p]
        b, l = code >> bits, code & (n_blocks - 1)
        s = jnp.dot(cat_ref[b], keys_sc[l], preferred_element_type=F32)
        s = (s + wide(self_ref[b], frames)) * shr_sc[l]
        score_sc[p] = s
        top_ref[b] = functools.reduce(jnp.maximum, lane_tiles(s), top_ref[b])

    unrolled(count, score)
    for b in range(n_blocks):
        top_ref[b] = jnp.broadcast_to(jnp.max(top_ref[b], axis=1, keepdims=True), (BS, LANES))
    values.wait()

    def read(p):
        code = pairs_ref[OWN_AT + p]
        b, l = code >> bits, code & (n_blocks - 1)
        w = jnp.exp2(score_sc[p] - wide(top_ref[b], frames))
        total_ref[b] = functools.reduce(jnp.add, lane_tiles(w), total_ref[b])
        v = value_sc[:, pl.ds(pl.multiple_of(l * BS, BS), BS), :].reshape(cols, value_width)
        acc_ref[b] += jnp.dot(w.astype(BF16), v, preferred_element_type=F32)

    unrolled(count, read)
    for copy in edges:
        copy.wait()


def gate(x_ref, *refs):
    pass

def halo_scores(
    sizes, pairs_ref, cat_ref, self_ref, chip_ref, link_ref, own_top_ref, own_total_ref,
    weight_ref, factor_ref, stats_ref,
    keys_sc, shr_sc, score_sc, top_sc, total_sc,
):
    frames, pixels, n_blocks, n_listed, key_width, value_width = sizes
    rows = frames * EDGE
    scale = -math.log2(math.e) / math.sqrt(key_width)
    for e in range(W):
        at = rows + e * key_width
        keys_sc[e] = squares_over(chip_ref[at : at + key_width, :])
        for f in range(frames):
            keys_sc[W + e, :, f * BS : (f + 1) * BS] = squares_over(link_ref[key_place(sizes, e, f)])
    shrinks = [
        chip_ref[rows + W * key_width :, :LANES].astype(F32) * scale,
        link_ref[link_ref.shape[0] - 16 :, :LANES].astype(F32) * scale,
    ]
    for side in range(2):
        for e in range(W):
            for f in range(frames):
                at = e * frames + f
                shr_sc[side * W + e, :, f * BS : (f + 1) * BS] = shrinks[side][at : at + 1, :]
    top_sc[...] = jnp.full_like(top_sc, NONE)
    total_sc[...] = jnp.zeros_like(total_sc)
    count = pairs_ref[COUNT_AT + 1]

    def score(p):
        code = pairs_ref[HALO_AT + p]
        b, h = code >> 2, code & 3
        s = jnp.dot(cat_ref[b], keys_sc[h], preferred_element_type=F32)
        s = (s + wide(self_ref[b], frames)) * shr_sc[h]
        score_sc[p] = s
        top_sc[b] = functools.reduce(jnp.maximum, lane_tiles(s), top_sc[b])

    unrolled(count, score)
    for b in range(n_blocks):
        own = own_top_ref[b]
        top = jnp.maximum(own, jnp.broadcast_to(jnp.max(top_sc[b], axis=1, keepdims=True), (BS, LANES)))
        top_sc[b] = top
        factor_ref[b] = jnp.exp2(own - top)

    def weigh(p):
        code = pairs_ref[HALO_AT + p]
        b = code >> 2
        w = jnp.exp2(score_sc[p] - wide(top_sc[b], frames))
        total_sc[b] = functools.reduce(jnp.add, lane_tiles(w), total_sc[b])
        weight_ref[p] = w.astype(BF16)

    unrolled(count, weigh)
    for b in range(n_blocks):
        total = jnp.sum(total_sc[b] + own_total_ref[b] * factor_ref[b], axis=1, keepdims=True)
        stats_ref[b : b + 1, :] = jnp.transpose(top_sc[b])[:1, :]
        stats_ref[n_blocks + b : n_blocks + b + 1, :] = jnp.transpose(jnp.broadcast_to(total, (BS, LANES)))[:1, :]


def chunk_sums(sizes, lanes, pairs_ref, weight_ref, acc_ref, factor_ref, stats_ref, chip_ref, link_ref, *refs):
    frames, pixels, n_blocks, n_listed, key_width, value_width = sizes
    cols = frames * BS
    out_ref, sum_sc = refs[-2:]
    width = lanes.stop - lanes.start
    for b in range(n_blocks):
        sum_sc[b] = acc_ref[b, :, lanes] * wide(factor_ref[b], width // LANES)
    sum_sc[n_blocks] = jnp.zeros((BS, width), F32)

    def add(p):
        code = pairs_ref[HALO_AT + p]
        b, h = code >> 2, code & 3
        at = pl.multiple_of((h & (W - 1)) * cols, cols)
        chip = chip_ref[pl.ds(at, cols), lanes]
        v = jnp.where(h >= W, link_ref[pl.ds(at, cols), :], chip)
        sum_sc[b] += jnp.dot(weight_ref[p], v, preferred_element_type=F32)

    unrolled(pairs_ref[COUNT_AT + 1], add)
    for b in range(n_blocks):
        out_ref[b * BS : (b + 1) * BS, :] = sum_sc[b].astype(BF16)
    if lanes.start == 0:
        rest = stats_ref[...]
        for i in range(3):
            piece = rest.astype(BF16)
            rest = rest - piece.astype(F32)
            out_ref[pixels + i * 2 * n_blocks : pixels + (i + 1) * 2 * n_blocks, :] = piece


def unpack_stats(x, n_blocks):
    n = 2 * n_blocks
    x = x.astype(F32)
    x = (x[:n] + x[n : 2 * n]) + x[2 * n :]
    return x[:n_blocks], x[n_blocks:]


def combine(sizes, *refs):
    frames, pixels, n_blocks = sizes[:3]
    n = len(refs) // 2
    mine, other, out_ref = refs[:n], refs[n : 2 * n], refs[-1]

    def run(first, second):
        top_a, total_a = unpack_stats(first[0][pixels:, :], n_blocks)
        top_b, total_b = unpack_stats(second[0][pixels:, :], n_blocks)
        top = jnp.maximum(top_a, top_b)
        a, b = jnp.exp2(top_a - top), jnp.exp2(top_b - top)
        total = total_a * a + total_b * b
        a, b = a / total, b / total
        for i in range(n_blocks):
            col_a = row_to_lanes(a[i : i + 1, :])
            col_b = row_to_lanes(b[i : i + 1, :])
            r = slice(i * BS, (i + 1) * BS)
            at = 0
            for one, two in zip(first, second):
                width = one.shape[1]
                times = width // LANES
                x = one[r, :].astype(F32) * wide(col_a, times) + two[r, :].astype(F32) * wide(col_b, times)
                out_ref[r, at : at + width] = x.astype(BF16)
                at += width

    me = lax.axis_index("tm")

    @pl.when(me == 0)
    def _():
        run(mine, other)

    @pl.when(me != 0)
    def _():
        run(other, mine)


def shards(n_space, n_tm, query_key, selection, memory_key, shrinkage, memory_value, block_list, block_count):
    frames, pixels, key_width = memory_key.shape
    value_width = memory_value.shape[2]
    n_blocks, n_listed = block_list.shape
    sizes = (frames, pixels, n_blocks, n_listed, key_width, value_width)
    cols = frames * BS
    rows = frames * EDGE
    n_chunks = value_width // WIDTH
    link_rows = rows + W * frames * key_width * LANES // WIDTH + 16
    chip_rows = rows + W * key_width + 16
    max_halo = n_blocks * min(n_listed, 2 * W) + UNROLL
    max_own = n_blocks * n_listed + UNROLL
    struct = jax.ShapeDtypeStruct
    dma = pltpu.SemaphoreType.DMA
    query, select = jnp.swapaxes(query_key[0], 0, 1), jnp.swapaxes(selection[0], 0, 1)
    keys = jnp.swapaxes(memory_key, 1, 2)
    query, select, keys, shrinkage, memory_value, block_list, block_count = [
        pltpu.with_memory_space_constraint(x, pltpu.HBM)
        for x in (query, select, keys, shrinkage, memory_value, block_list, block_count)
    ]
    on_chip = [(i ^ 1, i) for i in range(n_space)]
    over_link = []
    for i in range(n_space):
        for t in range(n_tm):
            j = i - 1 if i % 2 == 0 else i + 1
            source = j * n_tm + t if 0 <= j < n_space else i * n_tm + (t ^ 1)
            over_link.append((source, i * n_tm + t))
    round_link = [((i - 1 if i % 2 == 0 else i + 1) % n_space, i) for i in range(n_space)]
    swap = [(i ^ 1, i) for i in range(n_tm)]

    pairs, link_edge, chip_edge, query, select, keys, near_shrink = pl.pallas_call(
        functools.partial(lists_and_edge, sizes),
        out_shape=(
            struct((256,), jnp.int32),
            struct((link_rows, WIDTH), BF16),
            struct((chip_rows, value_width), BF16),
            struct(query.shape, BF16),
            struct(select.shape, BF16),
            struct(keys.shape, BF16),
            struct(shrinkage.shape, BF16),
        ),
        in_specs=[HBM] * 7,
        out_specs=(SMEM,) + (VMEM,) * 6,
        scratch_shapes=[
            pltpu.SMEM(block_list.shape, jnp.int32),
            pltpu.SMEM(block_count.shape, jnp.int32),
            dma((2, W * frames)),
            dma((2 * W * frames,)),
            dma((6,)),
        ],
        compiler_params=params(1),
        name="lists_and_edge",
    )(block_list, block_count, query, select, keys, shrinkage, memory_value)
    link_halo = [lax.ppermute(link_edge, ("space", "tm"), over_link)]
    chip_halo = lax.ppermute(chip_edge, "space", on_chip)

    acc, own_top, own_total, cat, self_term, *more_edges = pl.pallas_call(
        functools.partial(own_part, sizes),
        out_shape=(
            struct((n_blocks + 1, BS, value_width), F32),
            struct((n_blocks + 1, BS, LANES), F32),
            struct((n_blocks + 1, BS, LANES), F32),
            struct((n_blocks + 1, BS, 2 * key_width), BF16),
            struct((n_blocks + 1, BS, LANES), F32),
        )
        + (struct((rows, WIDTH), BF16),) * (n_chunks - 1),
        in_specs=[SMEM, VMEM, VMEM, VMEM, VMEM, HBM],
        out_specs=(VMEM,) * (4 + n_chunks),
        scratch_shapes=[
            pltpu.VMEM((n_blocks, 2 * key_width, cols), BF16),
            pltpu.VMEM((n_blocks, 1, cols), F32),
            pltpu.VMEM((max_own, BS, cols), F32),
            pltpu.VMEM(memory_value.shape, BF16),
            dma,
            dma((n_chunks - 1, W * frames)),
        ],
        compiler_params=params(24),
        name="own_part",
    )(pairs, query, select, keys, near_shrink, memory_value)
    def send_edge(edge, *after):
        edge = pl.pallas_call(
            gate,
            out_shape=struct(edge.shape, edge.dtype),
            in_specs=[VMEM] * (1 + len(after)),
            out_specs=VMEM,
            input_output_aliases={0: 0},
            compiler_params=params(1),
            name="gate",
        )(edge, *after)
        return lax.ppermute(edge, "space", round_link)

    link_halo.append(send_edge(more_edges[0], link_halo[0], own_top))

    weights, factor, stats = pl.pallas_call(
        functools.partial(halo_scores, sizes),
        out_shape=(
            struct((max_halo, BS, cols), BF16),
            struct((n_blocks + 1, BS, LANES), F32),
            struct((2 * n_blocks, LANES), F32),
        ),
        in_specs=[SMEM] + [VMEM] * 6,
        out_specs=(VMEM,) * 3,
        scratch_shapes=[
            pltpu.VMEM((2 * W, 2 * key_width, cols), BF16),
            pltpu.VMEM((2 * W, 1, cols), F32),
            pltpu.VMEM((max_halo, BS, cols), F32),
            pltpu.VMEM((n_blocks + 1, BS, LANES), F32),
            pltpu.VMEM((n_blocks + 1, BS, LANES), F32),
        ],
        compiler_params=params(12),
        name="halo_scores",
    )(pairs, cat, self_term, chip_halo, link_halo[0], own_top, own_total)

    mine, other = [], []
    for c in range(n_chunks):
        lanes = slice(c * WIDTH, (c + 1) * WIDTH)
        out_rows = pixels + (6 * n_blocks if c == 0 else 0)
        after = other[:1] if c == 2 else []
        x = pl.pallas_call(
            functools.partial(chunk_sums, sizes, lanes),
            out_shape=struct((out_rows, WIDTH), BF16),
            in_specs=[SMEM] + [VMEM] * (6 + len(after)),
            out_specs=VMEM,
            scratch_shapes=[pltpu.VMEM((n_blocks + 1, BS, WIDTH), F32)],
            compiler_params=params(4),
            name=f"chunk_sums_{c}",
        )(pairs, weights, acc, factor, stats, chip_halo, link_halo[c], *after)
        mine.append(x)
        if c + 2 < n_chunks:
            link_halo.append(send_edge(more_edges[c + 1], x))
        other.append(lax.ppermute(x, "tm", swap) if n_tm == 2 else lax.all_gather(x, "tm"))

    if n_tm == 2:
        out = pl.pallas_call(
            functools.partial(combine, sizes),
            out_shape=struct((pixels, value_width), BF16),
            in_specs=[VMEM] * len(mine + other),
            out_specs=VMEM,
            compiler_params=params(2),
            name="combine",
        )(*mine, *other)
    else:
        packed = other[0][:, pixels:, :]
        tops, totals = zip(*[unpack_stats(packed[i], n_blocks) for i in range(n_tm)])
        tops = jnp.stack(tops).reshape(n_tm, pixels, 1)
        totals = jnp.stack(totals).reshape(n_tm, pixels, 1)
        factors = jnp.exp2(tops - jnp.max(tops, axis=0, keepdims=True))
        total = jnp.sum(totals * factors, axis=0)
        sums = [jnp.sum(x[:, :pixels, :].astype(F32) * factors, axis=0) / total for x in other]
        out = jnp.concatenate(sums, axis=1).astype(BF16)
    return out[None]


def solution(mesh):
    in_specs = (
        P(None, "space", None),
        P(None, "space", None),
        P("tm", "space", None),
        P("tm", "space"),
        P("tm", "space", None),
        P("space", None),
        P("space"),
    )
    out_specs = P(None, "space", None)
    body = functools.partial(shards, mesh.shape["space"], mesh.shape["tm"])
    return jax.shard_map(body, mesh=mesh, in_specs=in_specs, out_specs=out_specs, check_vma=False)
```

```python
import functools
import math

import jax
import jax.numpy as jnp
from jax import lax
from jax.experimental import pallas as pl
from jax.experimental.pallas import tpu as pltpu
from jax.sharding import PartitionSpec as P

BS = 128
W = 2
LANES = 128
EDGE = W * BS
NONE = -1e30
WIDTH = 128
UNROLL = 8
OWN_AT, HALO_AT, COUNT_AT = 0, 64, 128
F32, BF16 = jnp.float32, jnp.bfloat16

VMEM = pl.BlockSpec(memory_space=pltpu.VMEM)
SMEM = pl.BlockSpec(memory_space=pltpu.SMEM)
HBM = pl.BlockSpec(memory_space=pltpu.HBM)


def params(mib):
    return pltpu.CompilerParams(vmem_limit_bytes=mib * 1024 * 1024)


def row_to_lanes(row):
    return jnp.transpose(jnp.broadcast_to(row, (row.shape[1], row.shape[1])))


def lane_tiles(x):
    return [x[:, i * LANES : (i + 1) * LANES] for i in range(x.shape[1] // LANES)]


def wide(x, times):
    return jnp.concatenate([x] * times, axis=1)


def value_copy(value_ref, out, start, lanes, sem):
    return pltpu.make_async_copy(value_ref.at[:, pl.ds(start, EDGE), lanes], out.at[:, pl.ds(0, EDGE), :], sem)


def edge_start(pixels, over_link):
    odd = lax.rem(lax.axis_index("space"), 2)
    side = odd if over_link else 1 - odd
    return pl.multiple_of(side * (pixels - EDGE), EDGE)


def shrink_rows(sizes, shrink, start):
    frames = sizes[0]
    edge = shrink[:, pl.ds(start, EDGE)].astype(F32)
    rows = [edge[:, e * BS : (e + 1) * BS] for e in range(W)]
    pad = jnp.zeros((16 - W * frames, LANES), F32)
    return jnp.concatenate(rows + [pad], axis=0).astype(BF16)


def lists_and_edge(
    sizes, list_ref, count_ref, query_ref, select_ref, key_ref, shrink_ref, value_ref,
    pairs_ref, link_ref, chip_ref, query_out, select_out, key_out, shrink_out,
    list_sc, count_sc, small_sems, sems,
):
    frames, pixels, n_blocks, n_listed, key_width, value_width = sizes
    start = edge_start(pixels, True)
    small = [
        pltpu.make_async_copy(list_ref, list_sc, small_sems.at[0]),
        pltpu.make_async_copy(count_ref, count_sc, small_sems.at[1]),
        pltpu.make_async_copy(shrink_ref, shrink_out, small_sems.at[2]),
    ]
    for copy in small:
        copy.start()
    chip_start = edge_start(pixels, False)
    copies = [value_copy(value_ref, link_ref, start, pl.ds(0, WIDTH), sems.at[0])]
    for e in range(W):
        copies.append(
            pltpu.make_async_copy(
                key_ref.at[:, :, pl.ds(start + e * BS, BS)],
                link_ref.at[:, pl.ds(EDGE + e * key_width, key_width), :],
                sems.at[1 + e],
            )
        )
    copies += [
        pltpu.make_async_copy(query_ref, query_out, sems.at[W + 1]),
        pltpu.make_async_copy(select_ref, select_out, sems.at[W + 2]),
        pltpu.make_async_copy(key_ref, key_out, sems.at[W + 3]),
        value_copy(value_ref, chip_ref, chip_start, slice(None), sems.at[W + 4]),
        pltpu.make_async_copy(
            key_ref.at[:, :, pl.ds(chip_start, EDGE)],
            chip_ref.at[:, pl.ds(EDGE, key_width), pl.ds(0, EDGE)],
            sems.at[W + 5],
        ),
    ]
    for copy in copies:
        copy.start()
    for copy in small:
        copy.wait()
    link_ref[0, EDGE + W * key_width :, :] = shrink_rows(sizes, shrink_out, start)
    chip_ref[0, EDGE + key_width :, :LANES] = shrink_rows(sizes, shrink_out, chip_start)
    odd = lax.rem(lax.axis_index("space"), 2)

    left, right = W * (1 - odd), W * odd - (W + n_blocks)

    def block(b, carry):
        n_own, n_halo = carry
        live = count_sc[b]
        for j in range(n_listed):
            l = list_sc[b, j]
            inside = (l >= W) & (l < W + n_blocks)
            pairs_ref[OWN_AT + n_own] = b * n_blocks + (l - W)
            pairs_ref[HALO_AT + n_halo] = b * 4 + l + jnp.where(l >= W, right, left)
            n_own += jnp.where((j < live) & inside, 1, 0)
            n_halo += jnp.where((j < live) & jnp.logical_not(inside), 1, 0)
        return n_own, n_halo

    n_own, n_halo = lax.fori_loop(0, n_blocks, block, (0, 0))
    for i in range(UNROLL - 1):
        pairs_ref[OWN_AT + n_own + i] = n_blocks * n_blocks
        pairs_ref[HALO_AT + n_halo + i] = n_blocks * 4
    pairs_ref[COUNT_AT] = n_own
    pairs_ref[COUNT_AT + 1] = n_halo
    for copy in copies:
        copy.wait()


def unrolled(count, body):
    def step(i, carry):
        for k in range(UNROLL):
            body(UNROLL * i + k)
        return carry

    lax.fori_loop(0, (count + UNROLL - 1) // UNROLL, step, 0)


def squares_over(k):
    k_f = k.astype(F32)
    return jnp.concatenate([(k_f * k_f).astype(BF16), k], axis=0)


def own_part(
    sizes, pairs_ref, query_ref, select_ref, key_ref, shrink_ref, value_ref,
    acc_ref, top_ref, total_ref, cat_ref, self_ref, *refs,
):
    links, (keys_sc, shr_sc, score_sc, value_sc, sem, edge_sems) = refs[:-6], refs[-6:]
    frames, pixels, n_blocks, n_listed, key_width, value_width = sizes
    cols = frames * BS
    bits = int(math.log2(n_blocks))
    values = pltpu.make_async_copy(value_ref, value_sc, sem)
    values.start()
    edges = []
    at = WIDTH
    for i, link in enumerate(links):
        lanes = pl.ds(at, link.shape[2])
        edges.append(value_copy(value_ref, link, edge_start(pixels, True), lanes, edge_sems.at[i]))
        at += link.shape[2]
    for copy in edges:
        copy.start()
    scale = -math.log2(math.e) / math.sqrt(key_width)
    for b in range(n_blocks):
        block = slice(b * BS, (b + 1) * BS)
        q = query_ref[:, block].astype(F32)
        s = select_ref[:, block].astype(F32)
        both = jnp.concatenate([s, -2.0 * q * s], axis=0)
        cat_ref[b] = jnp.transpose(both).astype(BF16)
        self_ref[b] = row_to_lanes(jnp.sum(s * q * q, axis=0, keepdims=True))
    cat_ref[n_blocks] = jnp.zeros((BS, 2 * key_width), BF16)
    self_ref[n_blocks] = jnp.zeros((BS, LANES), F32)
    shrink = shrink_ref[...].astype(F32) * scale
    for l in range(n_blocks):
        for f in range(frames):
            block = slice(l * BS, (l + 1) * BS)
            keys_sc[l, :, f * BS : (f + 1) * BS] = squares_over(key_ref[f, :, block])
            shr_sc[l, :, f * BS : (f + 1) * BS] = shrink[f : f + 1, block]
    top_ref[...] = jnp.full_like(top_ref, NONE)
    total_ref[...] = jnp.zeros_like(total_ref)
    acc_ref[...] = jnp.zeros_like(acc_ref)
    count = pairs_ref[COUNT_AT]

    def score(p):
        code = pairs_ref[OWN_AT + p]
        b, l = code >> bits, code & (n_blocks - 1)
        s = jnp.dot(cat_ref[b], keys_sc[l], preferred_element_type=F32)
        s = (s + wide(self_ref[b], frames)) * shr_sc[l]
        score_sc[p] = s
        top_ref[b] = functools.reduce(jnp.maximum, lane_tiles(s), top_ref[b])

    unrolled(count, score)
    for b in range(n_blocks):
        top_ref[b] = jnp.broadcast_to(jnp.max(top_ref[b], axis=1, keepdims=True), (BS, LANES))
    values.wait()

    def read(p):
        code = pairs_ref[OWN_AT + p]
        b, l = code >> bits, code & (n_blocks - 1)
        w = jnp.exp2(score_sc[p] - wide(top_ref[b], frames))
        total_ref[b] = functools.reduce(jnp.add, lane_tiles(w), total_ref[b])
        v = value_sc[:, pl.ds(pl.multiple_of(l * BS, BS), BS), :].reshape(cols, value_width)
        acc_ref[b] += jnp.dot(w.astype(BF16), v, preferred_element_type=F32)

    unrolled(count, read)
    for copy in edges:
        copy.wait()


def gate(x_ref, *refs):
    pass

def halo_scores(
    sizes, pairs_ref, cat_ref, self_ref, chip_ref, link_ref, own_top_ref, own_total_ref,
    weight_ref, factor_ref, stats_ref,
    keys_sc, shr_sc, score_sc, top_sc, total_sc,
):
    frames, pixels, n_blocks, n_listed, key_width, value_width = sizes
    scale = -math.log2(math.e) / math.sqrt(key_width)
    for e in range(W):
        at = EDGE + e * key_width
        for f in range(frames):
            place = slice(f * BS, (f + 1) * BS)
            keys_sc[e, :, place] = squares_over(chip_ref[f, EDGE : EDGE + key_width, e * BS : (e + 1) * BS])
            keys_sc[W + e, :, place] = squares_over(link_ref[f, at : at + key_width, :])
    shrinks = [
        chip_ref[0, EDGE + key_width :, :LANES].astype(F32) * scale,
        link_ref[0, EDGE + W * key_width :, :].astype(F32) * scale,
    ]
    for side in range(2):
        for e in range(W):
            for f in range(frames):
                at = e * frames + f
                shr_sc[side * W + e, :, f * BS : (f + 1) * BS] = shrinks[side][at : at + 1, :]
    top_sc[...] = jnp.full_like(top_sc, NONE)
    total_sc[...] = jnp.zeros_like(total_sc)
    count = pairs_ref[COUNT_AT + 1]

    def score(p):
        code = pairs_ref[HALO_AT + p]
        b, h = code >> 2, code & 3
        s = jnp.dot(cat_ref[b], keys_sc[h], preferred_element_type=F32)
        s = (s + wide(self_ref[b], frames)) * shr_sc[h]
        score_sc[p] = s
        top_sc[b] = functools.reduce(jnp.maximum, lane_tiles(s), top_sc[b])

    unrolled(count, score)
    for b in range(n_blocks):
        own = own_top_ref[b]
        top = jnp.maximum(own, jnp.broadcast_to(jnp.max(top_sc[b], axis=1, keepdims=True), (BS, LANES)))
        top_sc[b] = top
        factor_ref[b] = jnp.exp2(own - top)

    def weigh(p):
        code = pairs_ref[HALO_AT + p]
        b = code >> 2
        w = jnp.exp2(score_sc[p] - wide(top_sc[b], frames))
        total_sc[b] = functools.reduce(jnp.add, lane_tiles(w), total_sc[b])
        weight_ref[p] = w.astype(BF16)

    unrolled(count, weigh)
    for b in range(n_blocks):
        total = jnp.sum(total_sc[b] + own_total_ref[b] * factor_ref[b], axis=1, keepdims=True)
        stats_ref[b : b + 1, :] = jnp.transpose(top_sc[b])[:1, :]
        stats_ref[n_blocks + b : n_blocks + b + 1, :] = jnp.transpose(jnp.broadcast_to(total, (BS, LANES)))[:1, :]


def chunk_sums(sizes, lanes, begin, pairs_ref, weight_ref, acc_ref, factor_ref, stats_ref, chip_ref, link_ref, *refs):
    frames, pixels, n_blocks, n_listed, key_width, value_width = sizes
    cols = frames * BS
    out_ref, sum_sc = refs[-2:]
    width = lanes.stop - lanes.start
    for b in range(n_blocks):
        sum_sc[b] = acc_ref[b, :, lanes] * wide(factor_ref[b], width // LANES)
    sum_sc[n_blocks] = jnp.zeros((BS, width), F32)

    def add(p):
        code = pairs_ref[HALO_AT + p]
        b, h = code >> 2, code & 3
        rows = pl.ds(pl.multiple_of((h & (W - 1)) * BS, BS), BS)
        link = link_ref[:, rows, lanes.start - begin : lanes.stop - begin]
        v = jnp.where(h >= W, link, chip_ref[:, rows, lanes]).reshape(cols, width)
        sum_sc[b] += jnp.dot(weight_ref[p], v, preferred_element_type=F32)

    unrolled(pairs_ref[COUNT_AT + 1], add)
    for b in range(n_blocks):
        out_ref[b * BS : (b + 1) * BS, :] = sum_sc[b].astype(BF16)
    if lanes.start == 0:
        rest = stats_ref[...]
        for i in range(3):
            piece = rest.astype(BF16)
            rest = rest - piece.astype(F32)
            out_ref[pixels + i * 2 * n_blocks : pixels + (i + 1) * 2 * n_blocks, :] = piece


def unpack_stats(x, n_blocks):
    n = 2 * n_blocks
    x = x.astype(F32)
    x = (x[:n] + x[n : 2 * n]) + x[2 * n :]
    return x[:n_blocks], x[n_blocks:]


def combine(sizes, first_lane, count, *refs):
    frames, pixels, n_blocks, n_listed, key_width, value_width = sizes
    begin = first_lane == 0
    mine, other, refs = refs[:count], refs[count : 2 * count], refs[2 * count :]
    if begin:
        out_ref, cols_ref, out_sc, sem = refs
    else:
        cols_ref, before_ref, out_ref, out_sc, sem = refs

    def run(one, two):
        if begin:
            top_a, total_a = unpack_stats(one[0][pixels:, :], n_blocks)
            top_b, total_b = unpack_stats(two[0][pixels:, :], n_blocks)
            top = jnp.maximum(top_a, top_b)
            a, b = jnp.exp2(top_a - top), jnp.exp2(top_b - top)
            total = total_a * a + total_b * b
            a, b = a / total, b / total
        for i in range(n_blocks):
            r = slice(i * BS, (i + 1) * BS)
            if begin:
                cols_ref[0, r, :] = row_to_lanes(a[i : i + 1, :])
                cols_ref[1, r, :] = row_to_lanes(b[i : i + 1, :])
            for c in range(count):
                x = one[c][r, :].astype(F32) * cols_ref[0, r, :] + two[c][r, :].astype(F32) * cols_ref[1, r, :]
                out_sc[r, c * WIDTH : (c + 1) * WIDTH] = x.astype(BF16)

    me = lax.axis_index("tm")

    @pl.when(me == 0)
    def _():
        run(mine, other)

    @pl.when(me != 0)
    def _():
        run(other, mine)

    copy = pltpu.make_async_copy(out_sc, out_ref.at[:, pl.ds(first_lane, count * WIDTH)], sem)
    copy.start()
    copy.wait()


def shards(n_space, n_tm, query_key, selection, memory_key, shrinkage, memory_value, block_list, block_count):
    frames, pixels, key_width = memory_key.shape
    value_width = memory_value.shape[2]
    n_blocks, n_listed = block_list.shape
    sizes = (frames, pixels, n_blocks, n_listed, key_width, value_width)
    cols = frames * BS
    n_chunks = value_width // WIDTH
    link_rows = EDGE + W * key_width + 16
    chip_rows = EDGE + key_width + 16
    max_halo = n_blocks * min(n_listed, 2 * W) + UNROLL
    max_own = n_blocks * n_listed + UNROLL
    struct = jax.ShapeDtypeStruct
    dma = pltpu.SemaphoreType.DMA
    query, select = jnp.swapaxes(query_key[0], 0, 1), jnp.swapaxes(selection[0], 0, 1)
    keys = jnp.swapaxes(memory_key, 1, 2)
    query, select, keys, shrinkage, memory_value, block_list, block_count = [
        pltpu.with_memory_space_constraint(x, pltpu.HBM)
        for x in (query, select, keys, shrinkage, memory_value, block_list, block_count)
    ]
    on_chip = [(i ^ 1, i) for i in range(n_space)]
    over_link = []
    for i in range(n_space):
        for t in range(n_tm):
            j = i - 1 if i % 2 == 0 else i + 1
            source = j * n_tm + t if 0 <= j < n_space else i * n_tm + (t ^ 1)
            over_link.append((source, i * n_tm + t))
    round_link = [((i - 1 if i % 2 == 0 else i + 1) % n_space, i) for i in range(n_space)]
    swap = [(i ^ 1, i) for i in range(n_tm)]

    pairs, link_edge, chip_edge, query, select, keys, near_shrink = pl.pallas_call(
        functools.partial(lists_and_edge, sizes),
        out_shape=(
            struct((256,), jnp.int32),
            struct((frames, link_rows, WIDTH), BF16),
            struct((frames, chip_rows, value_width), BF16),
            struct(query.shape, BF16),
            struct(select.shape, BF16),
            struct(keys.shape, BF16),
            struct(shrinkage.shape, BF16),
        ),
        in_specs=[HBM] * 7,
        out_specs=(SMEM,) + (VMEM,) * 6,
        scratch_shapes=[
            pltpu.SMEM(block_list.shape, jnp.int32),
            pltpu.SMEM(block_count.shape, jnp.int32),
            dma((3,)),
            dma((W + 6,)),
        ],
        compiler_params=params(1),
        name="lists_and_edge",
    )(block_list, block_count, query, select, keys, shrinkage, memory_value)
    link_halo = [lax.ppermute(link_edge, ("space", "tm"), over_link)]
    chip_halo = lax.ppermute(chip_edge, "space", on_chip)

    acc, own_top, own_total, cat, self_term, *more_edges = pl.pallas_call(
        functools.partial(own_part, sizes),
        out_shape=(
            struct((n_blocks + 1, BS, value_width), F32),
            struct((n_blocks + 1, BS, LANES), F32),
            struct((n_blocks + 1, BS, LANES), F32),
            struct((n_blocks + 1, BS, 2 * key_width), BF16),
            struct((n_blocks + 1, BS, LANES), F32),
        )
        + (struct((frames, EDGE, value_width - 2 * WIDTH), BF16), struct((frames, EDGE, WIDTH), BF16)),
        in_specs=[SMEM, VMEM, VMEM, VMEM, VMEM, HBM],
        out_specs=(VMEM,) * 7,
        scratch_shapes=[
            pltpu.VMEM((n_blocks, 2 * key_width, cols), BF16),
            pltpu.VMEM((n_blocks, 1, cols), F32),
            pltpu.VMEM((max_own, BS, cols), F32),
            pltpu.VMEM(memory_value.shape, BF16),
            dma,
            dma((2,)),
        ],
        compiler_params=params(24),
        name="own_part",
    )(pairs, query, select, keys, near_shrink, memory_value)
    def send_edge(axes, pairs, edge, *after):
        edge = pl.pallas_call(
            gate,
            out_shape=struct(edge.shape, edge.dtype),
            in_specs=[VMEM] * (1 + len(after)),
            out_specs=VMEM,
            input_output_aliases={0: 0},
            compiler_params=params(1),
            name="gate",
        )(edge, *after)
        return lax.ppermute(edge, axes, pairs)

    link_halo.append(send_edge(("space", "tm"), over_link, more_edges[0], link_halo[0], own_top))

    weights, factor, stats = pl.pallas_call(
        functools.partial(halo_scores, sizes),
        out_shape=(
            struct((max_halo, BS, cols), BF16),
            struct((n_blocks + 1, BS, LANES), F32),
            struct((2 * n_blocks, LANES), F32),
        ),
        in_specs=[SMEM] + [VMEM] * 6,
        out_specs=(VMEM,) * 3,
        scratch_shapes=[
            pltpu.VMEM((2 * W, 2 * key_width, cols), BF16),
            pltpu.VMEM((2 * W, 1, cols), F32),
            pltpu.VMEM((max_halo, BS, cols), F32),
            pltpu.VMEM((n_blocks + 1, BS, LANES), F32),
            pltpu.VMEM((n_blocks + 1, BS, LANES), F32),
        ],
        compiler_params=params(12),
        name="halo_scores",
    )(pairs, cat, self_term, chip_halo, link_halo[0], own_top, own_total)

    mine, other = [], []
    for c in range(n_chunks):
        lanes = slice(c * WIDTH, (c + 1) * WIDTH)
        out_rows = pixels + (6 * n_blocks if c == 0 else 0)
        after = other[:1] if c == n_chunks - 1 else []
        part, begin = (0, 0) if c == 0 else (2, lanes.start) if c == n_chunks - 1 else (1, WIDTH)
        x = pl.pallas_call(
            functools.partial(chunk_sums, sizes, lanes, begin),
            out_shape=struct((out_rows, WIDTH), BF16),
            in_specs=[SMEM] + [VMEM] * (6 + len(after)),
            out_specs=VMEM,
            scratch_shapes=[pltpu.VMEM((n_blocks + 1, BS, WIDTH), F32)],
            compiler_params=params(4),
            name=f"chunk_sums_{c}",
        )(pairs, weights, acc, factor, stats, chip_halo, link_halo[part], *after)
        mine.append(x)
        if c == 0:
            link_halo.append(send_edge("space", round_link, more_edges[1], x))
        other.append(lax.ppermute(x, "tm", swap) if n_tm == 2 else lax.all_gather(x, "tm"))

    if n_tm == 2:
        n = n_chunks - 1
        out, cols = pl.pallas_call(
            functools.partial(combine, sizes, 0, n),
            out_shape=(pltpu.HBM((pixels, value_width), BF16), struct((2, pixels, LANES), F32)),
            in_specs=[VMEM] * (2 * n),
            out_specs=(HBM, VMEM),
            scratch_shapes=[pltpu.VMEM((pixels, n * WIDTH), BF16), dma],
            compiler_params=params(2),
            name="combine_first",
        )(*mine[:n], *other[:n])
        out = pl.pallas_call(
            functools.partial(combine, sizes, n * WIDTH, 1),
            out_shape=pltpu.HBM((pixels, value_width), BF16),
            in_specs=[VMEM] * 3 + [HBM],
            out_specs=HBM,
            input_output_aliases={3: 0},
            scratch_shapes=[pltpu.VMEM((pixels, WIDTH), BF16), dma],
            compiler_params=params(2),
            name="combine_last",
        )(mine[n], other[n], cols, out)
    else:
        packed = other[0][:, pixels:, :]
        tops, totals = zip(*[unpack_stats(packed[i], n_blocks) for i in range(n_tm)])
        tops = jnp.stack(tops).reshape(n_tm, pixels, 1)
        totals = jnp.stack(totals).reshape(n_tm, pixels, 1)
        factors = jnp.exp2(tops - jnp.max(tops, axis=0, keepdims=True))
        total = jnp.sum(totals * factors, axis=0)
        sums = [jnp.sum(x[:, :pixels, :].astype(F32) * factors, axis=0) / total for x in other]
        out = jnp.concatenate(sums, axis=1).astype(BF16)
    return out[None]


def solution(mesh):
    in_specs = (
        P(None, "space", None),
        P(None, "space", None),
        P("tm", "space", None),
        P("tm", "space"),
        P("tm", "space", None),
        P("space", None),
        P("space"),
    )
    out_specs = P(None, "space", None)
    body = functools.partial(shards, mesh.shape["space"], mesh.shape["tm"])
    return jax.shard_map(body, mesh=mesh, in_specs=in_specs, out_specs=out_specs, check_vma=False)
```

```python
import functools
import math

import jax
import jax.numpy as jnp
from jax import lax
from jax.experimental import pallas as pl
from jax.experimental.pallas import tpu as pltpu
from jax.sharding import PartitionSpec as P

BS = 128
W = 2
LANES = 128
EDGE = W * BS
NONE = -1e30
WIDTH = 128
UNROLL = 8
OWN_AT, HALO_AT, COUNT_AT = 0, 64, 128
F32, BF16 = jnp.float32, jnp.bfloat16

VMEM = pl.BlockSpec(memory_space=pltpu.VMEM)
SMEM = pl.BlockSpec(memory_space=pltpu.SMEM)
HBM = pl.BlockSpec(memory_space=pltpu.HBM)


def params(mib):
    return pltpu.CompilerParams(vmem_limit_bytes=mib * 1024 * 1024)


def row_to_lanes(row):
    return jnp.transpose(jnp.broadcast_to(row, (row.shape[1], row.shape[1])))


def lane_tiles(x):
    return [x[:, i * LANES : (i + 1) * LANES] for i in range(x.shape[1] // LANES)]


def wide(x, times):
    return jnp.concatenate([x] * times, axis=1)


def value_copy(value_ref, out, start, lanes, sem):
    return pltpu.make_async_copy(value_ref.at[:, pl.ds(start, EDGE), lanes], out.at[:, pl.ds(0, EDGE), :], sem)


def edge_start(pixels, over_link):
    odd = lax.rem(lax.axis_index("space"), 2)
    side = odd if over_link else 1 - odd
    return pl.multiple_of(side * (pixels - EDGE), EDGE)


def shrink_rows(sizes, shrink, start):
    frames = sizes[0]
    edge = shrink[:, pl.ds(start, EDGE)].astype(F32)
    rows = [edge[:, e * BS : (e + 1) * BS] for e in range(W)]
    pad = jnp.zeros((16 - W * frames, LANES), F32)
    return jnp.concatenate(rows + [pad], axis=0).astype(BF16)


def lists_and_edge(
    sizes, list_ref, count_ref, query_ref, select_ref, key_ref, shrink_ref, value_ref,
    pairs_ref, link_ref, chip_ref, cat_ref, self_ref, keys_ref, shr_ref,
    list_sc, count_sc, query_out, select_out, key_out, shrink_out, small_sems, sems,
):
    frames, pixels, n_blocks, n_listed, key_width, value_width = sizes
    start = edge_start(pixels, True)
    small = [
        pltpu.make_async_copy(list_ref, list_sc, small_sems.at[0]),
        pltpu.make_async_copy(count_ref, count_sc, small_sems.at[1]),
        pltpu.make_async_copy(shrink_ref, shrink_out, small_sems.at[2]),
    ]
    for copy in small:
        copy.start()
    chip_start = edge_start(pixels, False)
    copies = [value_copy(value_ref, link_ref, start, pl.ds(0, WIDTH), sems.at[0])]
    for e in range(W):
        copies.append(
            pltpu.make_async_copy(
                key_ref.at[:, :, pl.ds(start + e * BS, BS)],
                link_ref.at[:, pl.ds(EDGE + e * key_width, key_width), :],
                sems.at[1 + e],
            )
        )
    operands = [
        pltpu.make_async_copy(query_ref, query_out, sems.at[W + 1]),
        pltpu.make_async_copy(select_ref, select_out, sems.at[W + 2]),
        pltpu.make_async_copy(key_ref, key_out, sems.at[W + 3]),
    ]
    copies += [
        value_copy(value_ref, chip_ref, chip_start, slice(None), sems.at[W + 4]),
        pltpu.make_async_copy(
            key_ref.at[:, :, pl.ds(chip_start, EDGE)],
            chip_ref.at[:, pl.ds(EDGE, key_width), pl.ds(0, EDGE)],
            sems.at[W + 5],
        ),
    ]
    for copy in operands + copies:
        copy.start()
    for copy in small:
        copy.wait()
    link_ref[0, EDGE + W * key_width :, :] = shrink_rows(sizes, shrink_out, start)
    chip_ref[0, EDGE + key_width :, :LANES] = shrink_rows(sizes, shrink_out, chip_start)
    odd = lax.rem(lax.axis_index("space"), 2)

    left, right = W * (1 - odd), W * odd - (W + n_blocks)

    def block(b, carry):
        n_own, n_halo = carry
        live = count_sc[b]
        for j in range(n_listed):
            l = list_sc[b, j]
            inside = (l >= W) & (l < W + n_blocks)
            pairs_ref[OWN_AT + n_own] = b * n_blocks + (l - W)
            pairs_ref[HALO_AT + n_halo] = b * 4 + l + jnp.where(l >= W, right, left)
            n_own += jnp.where((j < live) & inside, 1, 0)
            n_halo += jnp.where((j < live) & jnp.logical_not(inside), 1, 0)
        return n_own, n_halo

    n_own, n_halo = lax.fori_loop(0, n_blocks, block, (0, 0))
    for i in range(UNROLL - 1):
        pairs_ref[OWN_AT + n_own + i] = n_blocks * n_blocks
        pairs_ref[HALO_AT + n_halo + i] = n_blocks * 4
    pairs_ref[COUNT_AT] = n_own
    pairs_ref[COUNT_AT + 1] = n_halo
    for copy in operands:
        copy.wait()
    scale = -math.log2(math.e) / math.sqrt(key_width)
    for b in range(n_blocks):
        block = slice(b * BS, (b + 1) * BS)
        q = query_out[:, block].astype(F32)
        s = select_out[:, block].astype(F32)
        both = jnp.concatenate([s, -2.0 * q * s], axis=0)
        cat_ref[b] = jnp.transpose(both).astype(BF16)
        self_ref[b] = row_to_lanes(jnp.sum(s * q * q, axis=0, keepdims=True))
    cat_ref[n_blocks] = jnp.zeros((BS, 2 * key_width), BF16)
    self_ref[n_blocks] = jnp.zeros((BS, LANES), F32)
    shrink = shrink_out[...].astype(F32) * scale
    for l in range(n_blocks):
        for f in range(frames):
            block = slice(l * BS, (l + 1) * BS)
            keys_ref[l, :, f * BS : (f + 1) * BS] = squares_over(key_out[f, :, block])
            shr_ref[l, :, f * BS : (f + 1) * BS] = shrink[f : f + 1, block]
    for copy in copies:
        copy.wait()


def unrolled(count, body):
    def step(i, carry):
        for k in range(UNROLL):
            body(UNROLL * i + k)
        return carry

    lax.fori_loop(0, (count + UNROLL - 1) // UNROLL, step, 0)


def squares_over(k):
    k_f = k.astype(F32)
    return jnp.concatenate([(k_f * k_f).astype(BF16), k], axis=0)


def own_part(
    sizes, pairs_ref, cat_ref, self_ref, keys_ref, shr_ref, value_ref, acc_ref, top_ref, total_ref, *refs
):
    links, (score_sc, value_sc, sem, edge_sems) = refs[:-4], refs[-4:]
    frames, pixels, n_blocks, n_listed, key_width, value_width = sizes
    cols = frames * BS
    bits = int(math.log2(n_blocks))
    values = pltpu.make_async_copy(value_ref, value_sc, sem)
    values.start()
    edges = []
    at = WIDTH
    for i, link in enumerate(links):
        lanes = pl.ds(at, link.shape[2])
        edges.append(value_copy(value_ref, link, edge_start(pixels, True), lanes, edge_sems.at[i]))
        at += link.shape[2]
    top_ref[...] = jnp.full_like(top_ref, NONE)
    total_ref[...] = jnp.zeros_like(total_ref)
    acc_ref[...] = jnp.zeros_like(acc_ref)
    count = pairs_ref[COUNT_AT]

    def score(p):
        code = pairs_ref[OWN_AT + p]
        b, l = code >> bits, code & (n_blocks - 1)
        s = jnp.dot(cat_ref[b], keys_ref[l], preferred_element_type=F32)
        s = (s + wide(self_ref[b], frames)) * shr_ref[l]
        score_sc[p] = s
        top_ref[b] = functools.reduce(jnp.maximum, lane_tiles(s), top_ref[b])

    unrolled(count, score)
    for b in range(n_blocks):
        top_ref[b] = jnp.broadcast_to(jnp.max(top_ref[b], axis=1, keepdims=True), (BS, LANES))
    values.wait()
    for copy in edges:
        copy.start()

    def read(p):
        code = pairs_ref[OWN_AT + p]
        b, l = code >> bits, code & (n_blocks - 1)
        w = jnp.exp2(score_sc[p] - wide(top_ref[b], frames))
        total_ref[b] = functools.reduce(jnp.add, lane_tiles(w), total_ref[b])
        v = value_sc[:, pl.ds(pl.multiple_of(l * BS, BS), BS), :].reshape(cols, value_width)
        acc_ref[b] += jnp.dot(w.astype(BF16), v, preferred_element_type=F32)

    unrolled(count, read)
    for copy in edges:
        copy.wait()


def gate(x_ref, *refs):
    pass

def halo_scores(
    sizes, pairs_ref, cat_ref, self_ref, chip_ref, link_ref, own_top_ref, own_total_ref,
    weight_ref, factor_ref, stats_ref,
    keys_sc, shr_sc, score_sc, top_sc, total_sc,
):
    frames, pixels, n_blocks, n_listed, key_width, value_width = sizes
    scale = -math.log2(math.e) / math.sqrt(key_width)
    for e in range(W):
        at = EDGE + e * key_width
        for f in range(frames):
            place = slice(f * BS, (f + 1) * BS)
            keys_sc[e, :, place] = squares_over(chip_ref[f, EDGE : EDGE + key_width, e * BS : (e + 1) * BS])
            keys_sc[W + e, :, place] = squares_over(link_ref[f, at : at + key_width, :])
    shrinks = [
        chip_ref[0, EDGE + key_width :, :LANES].astype(F32) * scale,
        link_ref[0, EDGE + W * key_width :, :].astype(F32) * scale,
    ]
    for side in range(2):
        for e in range(W):
            for f in range(frames):
                at = e * frames + f
                shr_sc[side * W + e, :, f * BS : (f + 1) * BS] = shrinks[side][at : at + 1, :]
    top_sc[...] = jnp.full_like(top_sc, NONE)
    total_sc[...] = jnp.zeros_like(total_sc)
    count = pairs_ref[COUNT_AT + 1]

    def score(p):
        code = pairs_ref[HALO_AT + p]
        b, h = code >> 2, code & 3
        s = jnp.dot(cat_ref[b], keys_sc[h], preferred_element_type=F32)
        s = (s + wide(self_ref[b], frames)) * shr_sc[h]
        score_sc[p] = s
        top_sc[b] = functools.reduce(jnp.maximum, lane_tiles(s), top_sc[b])

    unrolled(count, score)
    for b in range(n_blocks):
        own = own_top_ref[b]
        top = jnp.maximum(own, jnp.broadcast_to(jnp.max(top_sc[b], axis=1, keepdims=True), (BS, LANES)))
        top_sc[b] = top
        factor_ref[b] = jnp.exp2(own - top)

    def weigh(p):
        code = pairs_ref[HALO_AT + p]
        b = code >> 2
        w = jnp.exp2(score_sc[p] - wide(top_sc[b], frames))
        total_sc[b] = functools.reduce(jnp.add, lane_tiles(w), total_sc[b])
        weight_ref[p] = w.astype(BF16)

    unrolled(count, weigh)
    for b in range(n_blocks):
        total = jnp.sum(total_sc[b] + own_total_ref[b] * factor_ref[b], axis=1, keepdims=True)
        stats_ref[b : b + 1, :] = jnp.transpose(top_sc[b])[:1, :]
        stats_ref[n_blocks + b : n_blocks + b + 1, :] = jnp.transpose(jnp.broadcast_to(total, (BS, LANES)))[:1, :]


def chunk_sums(sizes, lanes, begin, pairs_ref, weight_ref, acc_ref, factor_ref, stats_ref, chip_ref, link_ref, *refs):
    frames, pixels, n_blocks, n_listed, key_width, value_width = sizes
    cols = frames * BS
    out_ref, sum_sc = refs[-2:]
    width = lanes.stop - lanes.start
    for b in range(n_blocks):
        sum_sc[b] = acc_ref[b, :, lanes] * wide(factor_ref[b], width // LANES)
    sum_sc[n_blocks] = jnp.zeros((BS, width), F32)

    def add(p):
        code = pairs_ref[HALO_AT + p]
        b, h = code >> 2, code & 3
        rows = pl.ds(pl.multiple_of((h & (W - 1)) * BS, BS), BS)
        link = link_ref[:, rows, lanes.start - begin : lanes.stop - begin]
        v = jnp.where(h >= W, link, chip_ref[:, rows, lanes]).reshape(cols, width)
        sum_sc[b] += jnp.dot(weight_ref[p], v, preferred_element_type=F32)

    unrolled(pairs_ref[COUNT_AT + 1], add)
    for b in range(n_blocks):
        out_ref[b * BS : (b + 1) * BS, :] = sum_sc[b].astype(BF16)
    if lanes.start == 0:
        rest = stats_ref[...]
        for i in range(3):
            piece = rest.astype(BF16)
            rest = rest - piece.astype(F32)
            out_ref[pixels + i * 2 * n_blocks : pixels + (i + 1) * 2 * n_blocks, :] = piece


def unpack_stats(x, n_blocks):
    n = 2 * n_blocks
    x = x.astype(F32)
    x = (x[:n] + x[n : 2 * n]) + x[2 * n :]
    return x[:n_blocks], x[n_blocks:]


def combine(sizes, first_lane, count, *refs):
    frames, pixels, n_blocks, n_listed, key_width, value_width = sizes
    begin = first_lane == 0
    mine, other, refs = refs[:count], refs[count : 2 * count], refs[2 * count :]
    if begin:
        out_ref, cols_ref, out_sc, sem = refs
    else:
        cols_ref, before_ref, out_ref, out_sc, sem = refs

    def run(one, two):
        if begin:
            top_a, total_a = unpack_stats(one[0][pixels:, :], n_blocks)
            top_b, total_b = unpack_stats(two[0][pixels:, :], n_blocks)
            top = jnp.maximum(top_a, top_b)
            a, b = jnp.exp2(top_a - top), jnp.exp2(top_b - top)
            total = total_a * a + total_b * b
            a, b = a / total, b / total
        for i in range(n_blocks):
            r = slice(i * BS, (i + 1) * BS)
            if begin:
                cols_ref[0, r, :] = row_to_lanes(a[i : i + 1, :])
                cols_ref[1, r, :] = row_to_lanes(b[i : i + 1, :])
            for c in range(count):
                x = one[c][r, :].astype(F32) * cols_ref[0, r, :] + two[c][r, :].astype(F32) * cols_ref[1, r, :]
                out_sc[r, c * WIDTH : (c + 1) * WIDTH] = x.astype(BF16)

    me = lax.axis_index("tm")

    @pl.when(me == 0)
    def _():
        run(mine, other)

    @pl.when(me != 0)
    def _():
        run(other, mine)

    copy = pltpu.make_async_copy(out_sc, out_ref.at[:, pl.ds(first_lane, count * WIDTH)], sem)
    copy.start()
    copy.wait()


def shards(n_space, n_tm, query_key, selection, memory_key, shrinkage, memory_value, block_list, block_count):
    frames, pixels, key_width = memory_key.shape
    value_width = memory_value.shape[2]
    n_blocks, n_listed = block_list.shape
    sizes = (frames, pixels, n_blocks, n_listed, key_width, value_width)
    cols = frames * BS
    n_chunks = value_width // WIDTH
    link_rows = EDGE + W * key_width + 16
    chip_rows = EDGE + key_width + 16
    max_halo = n_blocks * min(n_listed, 2 * W) + UNROLL
    max_own = n_blocks * n_listed + UNROLL
    struct = jax.ShapeDtypeStruct
    dma = pltpu.SemaphoreType.DMA
    query, select = jnp.swapaxes(query_key[0], 0, 1), jnp.swapaxes(selection[0], 0, 1)
    keys = jnp.swapaxes(memory_key, 1, 2)
    query, select, keys, shrinkage, memory_value, block_list, block_count = [
        pltpu.with_memory_space_constraint(x, pltpu.HBM)
        for x in (query, select, keys, shrinkage, memory_value, block_list, block_count)
    ]
    on_chip = [(i ^ 1, i) for i in range(n_space)]
    over_link = []
    for i in range(n_space):
        for t in range(n_tm):
            j = i - 1 if i % 2 == 0 else i + 1
            source = j * n_tm + t if 0 <= j < n_space else i * n_tm + (t ^ 1)
            over_link.append((source, i * n_tm + t))
    round_link = [((i - 1 if i % 2 == 0 else i + 1) % n_space, i) for i in range(n_space)]
    swap = [(i ^ 1, i) for i in range(n_tm)]

    pairs, link_edge, chip_edge, cat, self_term, near_keys, near_shrink = pl.pallas_call(
        functools.partial(lists_and_edge, sizes),
        out_shape=(
            struct((256,), jnp.int32),
            struct((frames, link_rows, WIDTH), BF16),
            struct((frames, chip_rows, value_width), BF16),
            struct((n_blocks + 1, BS, 2 * key_width), BF16),
            struct((n_blocks + 1, BS, LANES), F32),
            struct((n_blocks, 2 * key_width, cols), BF16),
            struct((n_blocks, 1, cols), F32),
        ),
        in_specs=[HBM] * 7,
        out_specs=(SMEM,) + (VMEM,) * 6,
        scratch_shapes=[
            pltpu.SMEM(block_list.shape, jnp.int32),
            pltpu.SMEM(block_count.shape, jnp.int32),
            pltpu.VMEM(query.shape, BF16),
            pltpu.VMEM(select.shape, BF16),
            pltpu.VMEM(keys.shape, BF16),
            pltpu.VMEM(shrinkage.shape, BF16),
            dma((3,)),
            dma((W + 6,)),
        ],
        compiler_params=params(4),
        name="lists_and_edge",
    )(block_list, block_count, query, select, keys, shrinkage, memory_value)
    link_halo = [lax.ppermute(link_edge, ("space", "tm"), over_link)]
    chip_halo = lax.ppermute(chip_edge, "space", on_chip)

    acc, own_top, own_total, *more_edges = pl.pallas_call(
        functools.partial(own_part, sizes),
        out_shape=(
            struct((n_blocks + 1, BS, value_width), F32),
            struct((n_blocks + 1, BS, LANES), F32),
            struct((n_blocks + 1, BS, LANES), F32),
        )
        + (struct((frames, EDGE, value_width - 2 * WIDTH), BF16), struct((frames, EDGE, WIDTH), BF16)),
        in_specs=[SMEM, VMEM, VMEM, VMEM, VMEM, HBM],
        out_specs=(VMEM,) * 5,
        scratch_shapes=[
            pltpu.VMEM((max_own, BS, cols), F32),
            pltpu.VMEM(memory_value.shape, BF16),
            dma,
            dma((2,)),
        ],
        compiler_params=params(24),
        name="own_part",
    )(pairs, cat, self_term, near_keys, near_shrink, memory_value)
    def send_edge(axes, pairs, edge, *after):
        edge = pl.pallas_call(
            gate,
            out_shape=struct(edge.shape, edge.dtype),
            in_specs=[VMEM] * (1 + len(after)),
            out_specs=VMEM,
            input_output_aliases={0: 0},
            compiler_params=params(1),
            name="gate",
        )(edge, *after)
        return lax.ppermute(edge, axes, pairs)

    link_halo.append(send_edge(("space", "tm"), over_link, more_edges[0], link_halo[0], own_top))

    weights, factor, stats = pl.pallas_call(
        functools.partial(halo_scores, sizes),
        out_shape=(
            struct((max_halo, BS, cols), BF16),
            struct((n_blocks + 1, BS, LANES), F32),
            struct((2 * n_blocks, LANES), F32),
        ),
        in_specs=[SMEM] + [VMEM] * 6,
        out_specs=(VMEM,) * 3,
        scratch_shapes=[
            pltpu.VMEM((2 * W, 2 * key_width, cols), BF16),
            pltpu.VMEM((2 * W, 1, cols), F32),
            pltpu.VMEM((max_halo, BS, cols), F32),
            pltpu.VMEM((n_blocks + 1, BS, LANES), F32),
            pltpu.VMEM((n_blocks + 1, BS, LANES), F32),
        ],
        compiler_params=params(12),
        name="halo_scores",
    )(pairs, cat, self_term, chip_halo, link_halo[0], own_top, own_total)

    mine, other = [], []
    for c in range(n_chunks):
        lanes = slice(c * WIDTH, (c + 1) * WIDTH)
        out_rows = pixels + (6 * n_blocks if c == 0 else 0)
        after = other[:1] if c == n_chunks - 1 else []
        part, begin = (0, 0) if c == 0 else (2, lanes.start) if c == n_chunks - 1 else (1, WIDTH)
        x = pl.pallas_call(
            functools.partial(chunk_sums, sizes, lanes, begin),
            out_shape=struct((out_rows, WIDTH), BF16),
            in_specs=[SMEM] + [VMEM] * (6 + len(after)),
            out_specs=VMEM,
            scratch_shapes=[pltpu.VMEM((n_blocks + 1, BS, WIDTH), F32)],
            compiler_params=params(4),
            name=f"chunk_sums_{c}",
        )(pairs, weights, acc, factor, stats, chip_halo, link_halo[part], *after)
        mine.append(x)
        if c == 0:
            link_halo.append(send_edge("space", round_link, more_edges[1], x))
        other.append(lax.ppermute(x, "tm", swap) if n_tm == 2 else lax.all_gather(x, "tm"))

    if n_tm == 2:
        n = n_chunks - 1
        out, cols = pl.pallas_call(
            functools.partial(combine, sizes, 0, n),
            out_shape=(pltpu.HBM((pixels, value_width), BF16), struct((2, pixels, LANES), F32)),
            in_specs=[VMEM] * (2 * n),
            out_specs=(HBM, VMEM),
            scratch_shapes=[pltpu.VMEM((pixels, n * WIDTH), BF16), dma],
            compiler_params=params(2),
            name="combine_first",
        )(*mine[:n], *other[:n])
        out = pl.pallas_call(
            functools.partial(combine, sizes, n * WIDTH, 1),
            out_shape=pltpu.HBM((pixels, value_width), BF16),
            in_specs=[VMEM] * 3 + [HBM],
            out_specs=HBM,
            input_output_aliases={3: 0},
            scratch_shapes=[pltpu.VMEM((pixels, WIDTH), BF16), dma],
            compiler_params=params(2),
            name="combine_last",
        )(mine[n], other[n], cols, out)
    else:
        packed = other[0][:, pixels:, :]
        tops, totals = zip(*[unpack_stats(packed[i], n_blocks) for i in range(n_tm)])
        tops = jnp.stack(tops).reshape(n_tm, pixels, 1)
        totals = jnp.stack(totals).reshape(n_tm, pixels, 1)
        factors = jnp.exp2(tops - jnp.max(tops, axis=0, keepdims=True))
        total = jnp.sum(totals * factors, axis=0)
        sums = [jnp.sum(x[:, :pixels, :].astype(F32) * factors, axis=0) / total for x in other]
        out = jnp.concatenate(sums, axis=1).astype(BF16)
    return out[None]


def solution(mesh):
    in_specs = (
        P(None, "space", None),
        P(None, "space", None),
        P("tm", "space", None),
        P("tm", "space"),
        P("tm", "space", None),
        P("space", None),
        P("space"),
    )
    out_specs = P(None, "space", None)
    body = functools.partial(shards, mesh.shape["space"], mesh.shape["tm"])
    return jax.shard_map(body, mesh=mesh, in_specs=in_specs, out_specs=out_specs, check_vma=False)
```

```python
import functools
import math

import jax
import jax.numpy as jnp
from jax import lax
from jax.experimental import pallas as pl
from jax.experimental.pallas import tpu as pltpu
from jax.sharding import PartitionSpec as P

BS = 128
W = 2
LANES = 128
EDGE = W * BS
NONE = -1e30
WIDTH = 128
UNROLL = 8
OWN_AT, HALO_AT, COUNT_AT = 0, 64, 128
F32, BF16 = jnp.float32, jnp.bfloat16

VMEM = pl.BlockSpec(memory_space=pltpu.VMEM)
SMEM = pl.BlockSpec(memory_space=pltpu.SMEM)
HBM = pl.BlockSpec(memory_space=pltpu.HBM)


def params(mib):
    return pltpu.CompilerParams(vmem_limit_bytes=mib * 1024 * 1024)


def row_to_lanes(row):
    return jnp.transpose(jnp.broadcast_to(row, (row.shape[1], row.shape[1])))


def lane_tiles(x):
    return [x[:, i * LANES : (i + 1) * LANES] for i in range(x.shape[1] // LANES)]


def wide(x, times):
    return jnp.concatenate([x] * times, axis=1)


def value_copy(value_ref, out, start, lanes, sem):
    return pltpu.make_async_copy(value_ref.at[:, pl.ds(start, EDGE), lanes], out.at[:, pl.ds(0, EDGE), :], sem)


def edge_start(pixels, over_link):
    odd = lax.rem(lax.axis_index("space"), 2)
    side = odd if over_link else 1 - odd
    return pl.multiple_of(side * (pixels - EDGE), EDGE)


def shrink_rows(sizes, shrink, start):
    frames = sizes[0]
    edge = shrink[:, pl.ds(start, EDGE)].astype(F32)
    rows = [edge[:, e * BS : (e + 1) * BS] for e in range(W)]
    pad = jnp.zeros((16 - W * frames, LANES), F32)
    return jnp.concatenate(rows + [pad], axis=0).astype(BF16)


def lists_and_edge(
    sizes, list_ref, count_ref, query_ref, select_ref, key_ref, shrink_ref, value_ref,
    pairs_ref, link_ref, chip_ref, cat_ref, self_ref, keys_ref, shr_ref,
    list_sc, count_sc, query_out, select_out, key_out, shrink_out, small_sems, sems,
):
    frames, pixels, n_blocks, n_listed, key_width, value_width = sizes
    start = edge_start(pixels, True)
    small = [
        pltpu.make_async_copy(list_ref, list_sc, small_sems.at[0]),
        pltpu.make_async_copy(count_ref, count_sc, small_sems.at[1]),
        pltpu.make_async_copy(shrink_ref, shrink_out, small_sems.at[2]),
    ]
    for copy in small:
        copy.start()
    chip_start = edge_start(pixels, False)
    copies = [value_copy(value_ref, link_ref, start, pl.ds(0, WIDTH), sems.at[0])]
    for e in range(W):
        copies.append(
            pltpu.make_async_copy(
                key_ref.at[:, :, pl.ds(start + e * BS, BS)],
                link_ref.at[:, pl.ds(EDGE + e * key_width, key_width), :],
                sems.at[1 + e],
            )
        )
    operands = [
        pltpu.make_async_copy(query_ref, query_out, sems.at[W + 1]),
        pltpu.make_async_copy(select_ref, select_out, sems.at[W + 2]),
        pltpu.make_async_copy(key_ref, key_out, sems.at[W + 3]),
    ]
    copies += [
        value_copy(value_ref, chip_ref, chip_start, slice(None), sems.at[W + 4]),
        pltpu.make_async_copy(
            key_ref.at[:, :, pl.ds(chip_start, EDGE)],
            chip_ref.at[:, pl.ds(EDGE, key_width), pl.ds(0, EDGE)],
            sems.at[W + 5],
        ),
    ]
    for copy in operands + copies:
        copy.start()
    for copy in small:
        copy.wait()
    link_ref[0, EDGE + W * key_width :, :] = shrink_rows(sizes, shrink_out, start)
    chip_ref[0, EDGE + key_width :, :LANES] = shrink_rows(sizes, shrink_out, chip_start)
    odd = lax.rem(lax.axis_index("space"), 2)

    left, right = W * (1 - odd), W * odd - (W + n_blocks)

    def block(b, carry):
        n_own, n_halo = carry
        live = count_sc[b]
        for j in range(n_listed):
            l = list_sc[b, j]
            inside = (l >= W) & (l < W + n_blocks)
            pairs_ref[OWN_AT + n_own] = b * n_blocks + (l - W)
            pairs_ref[HALO_AT + n_halo] = b * 4 + l + jnp.where(l >= W, right, left)
            n_own += jnp.where((j < live) & inside, 1, 0)
            n_halo += jnp.where((j < live) & jnp.logical_not(inside), 1, 0)
        return n_own, n_halo

    n_own, n_halo = lax.fori_loop(0, n_blocks, block, (0, 0))
    for i in range(UNROLL - 1):
        pairs_ref[OWN_AT + n_own + i] = n_blocks * n_blocks
        pairs_ref[HALO_AT + n_halo + i] = n_blocks * 4
    pairs_ref[COUNT_AT] = n_own
    pairs_ref[COUNT_AT + 1] = n_halo
    for copy in operands:
        copy.wait()
    scale = -math.log2(math.e) / math.sqrt(key_width)
    for b in range(n_blocks):
        block = slice(b * BS, (b + 1) * BS)
        q = query_out[:, block].astype(F32)
        s = select_out[:, block].astype(F32)
        both = jnp.concatenate([s, -2.0 * q * s], axis=0)
        cat_ref[b] = jnp.transpose(both).astype(BF16)
        self_ref[b] = row_to_lanes(jnp.sum(s * q * q, axis=0, keepdims=True))
    cat_ref[n_blocks] = jnp.zeros((BS, 2 * key_width), BF16)
    self_ref[n_blocks] = jnp.zeros((BS, LANES), F32)
    shrink = shrink_out[...].astype(F32) * scale
    for l in range(n_blocks):
        for f in range(frames):
            block = slice(l * BS, (l + 1) * BS)
            keys_ref[l, :, f * BS : (f + 1) * BS] = squares_over(key_out[f, :, block])
            shr_ref[l, :, f * BS : (f + 1) * BS] = shrink[f : f + 1, block]
    for copy in copies:
        copy.wait()


def unrolled(count, body):
    def step(i, carry):
        for k in range(UNROLL):
            body(UNROLL * i + k)
        return carry

    lax.fori_loop(0, (count + UNROLL - 1) // UNROLL, step, 0)


def squares_over(k):
    k_f = k.astype(F32)
    return jnp.concatenate([(k_f * k_f).astype(BF16), k], axis=0)


def own_part(
    sizes, pairs_ref, cat_ref, self_ref, keys_ref, shr_ref, value_ref, acc_ref, top_ref, total_ref, *refs
):
    links, (score_sc, value_sc, sem, edge_sems) = refs[:-4], refs[-4:]
    frames, pixels, n_blocks, n_listed, key_width, value_width = sizes
    cols = frames * BS
    bits = int(math.log2(n_blocks))
    values = pltpu.make_async_copy(value_ref, value_sc, sem)
    values.start()
    edges = []
    at = WIDTH
    for i, link in enumerate(links):
        lanes = pl.ds(at, link.shape[2])
        edges.append(value_copy(value_ref, link, edge_start(pixels, True), lanes, edge_sems.at[i]))
        at += link.shape[2]
    top_ref[...] = jnp.full_like(top_ref, NONE)
    total_ref[...] = jnp.zeros_like(total_ref)
    acc_ref[...] = jnp.zeros_like(acc_ref)
    count = pairs_ref[COUNT_AT]

    def score(p):
        code = pairs_ref[OWN_AT + p]
        b, l = code >> bits, code & (n_blocks - 1)
        s = jnp.dot(cat_ref[b], keys_ref[l], preferred_element_type=F32)
        s = (s + wide(self_ref[b], frames)) * shr_ref[l]
        score_sc[p] = s
        top_ref[b] = functools.reduce(jnp.maximum, lane_tiles(s), top_ref[b])

    unrolled(count, score)
    for b in range(n_blocks):
        top_ref[b] = jnp.broadcast_to(jnp.max(top_ref[b], axis=1, keepdims=True), (BS, LANES))
    values.wait()
    for copy in edges:
        copy.start()

    def read(p):
        code = pairs_ref[OWN_AT + p]
        b, l = code >> bits, code & (n_blocks - 1)
        w = jnp.exp2(score_sc[p] - wide(top_ref[b], frames))
        total_ref[b] = functools.reduce(jnp.add, lane_tiles(w), total_ref[b])
        v = value_sc[:, pl.ds(pl.multiple_of(l * BS, BS), BS), :].reshape(cols, value_width)
        acc_ref[b] += jnp.dot(w.astype(BF16), v, preferred_element_type=F32)

    unrolled(count, read)
    for copy in edges:
        copy.wait()


def gate(x_ref, *refs):
    pass

def halo_scores(
    sizes, pairs_ref, cat_ref, self_ref, chip_ref, link_ref, own_top_ref, own_total_ref,
    weight_ref, factor_ref, stats_ref,
    keys_sc, shr_sc, score_sc, top_sc, total_sc,
):
    frames, pixels, n_blocks, n_listed, key_width, value_width = sizes
    scale = -math.log2(math.e) / math.sqrt(key_width)
    for e in range(W):
        at = EDGE + e * key_width
        for f in range(frames):
            place = slice(f * BS, (f + 1) * BS)
            keys_sc[e, :, place] = squares_over(chip_ref[f, EDGE : EDGE + key_width, e * BS : (e + 1) * BS])
            keys_sc[W + e, :, place] = squares_over(link_ref[f, at : at + key_width, :])
    shrinks = [
        chip_ref[0, EDGE + key_width :, :LANES].astype(F32) * scale,
        link_ref[0, EDGE + W * key_width :, :].astype(F32) * scale,
    ]
    for side in range(2):
        for e in range(W):
            for f in range(frames):
                at = e * frames + f
                shr_sc[side * W + e, :, f * BS : (f + 1) * BS] = shrinks[side][at : at + 1, :]
    top_sc[...] = jnp.full_like(top_sc, NONE)
    total_sc[...] = jnp.zeros_like(total_sc)
    count = pairs_ref[COUNT_AT + 1]

    def score(p):
        code = pairs_ref[HALO_AT + p]
        b, h = code >> 2, code & 3
        s = jnp.dot(cat_ref[b], keys_sc[h], preferred_element_type=F32)
        s = (s + wide(self_ref[b], frames)) * shr_sc[h]
        score_sc[p] = s
        top_sc[b] = functools.reduce(jnp.maximum, lane_tiles(s), top_sc[b])

    unrolled(count, score)
    for b in range(n_blocks):
        own = own_top_ref[b]
        top = jnp.maximum(own, jnp.broadcast_to(jnp.max(top_sc[b], axis=1, keepdims=True), (BS, LANES)))
        top_sc[b] = top
        factor_ref[b] = jnp.exp2(own - top)

    def weigh(p):
        code = pairs_ref[HALO_AT + p]
        b = code >> 2
        w = jnp.exp2(score_sc[p] - wide(top_sc[b], frames))
        total_sc[b] = functools.reduce(jnp.add, lane_tiles(w), total_sc[b])
        weight_ref[p] = w.astype(BF16)

    unrolled(count, weigh)
    for b in range(n_blocks):
        total = jnp.sum(total_sc[b] + own_total_ref[b] * factor_ref[b], axis=1, keepdims=True)
        stats_ref[b : b + 1, :] = jnp.transpose(top_sc[b])[:1, :]
        stats_ref[n_blocks + b : n_blocks + b + 1, :] = jnp.transpose(jnp.broadcast_to(total, (BS, LANES)))[:1, :]


def chunk_sums(sizes, lanes, begin, pairs_ref, weight_ref, acc_ref, factor_ref, stats_ref, chip_ref, link_ref, *refs):
    frames, pixels, n_blocks, n_listed, key_width, value_width = sizes
    cols = frames * BS
    out_ref, sum_sc = refs[-2:]
    width = lanes.stop - lanes.start
    for b in range(n_blocks):
        sum_sc[b] = acc_ref[b, :, lanes] * wide(factor_ref[b], width // LANES)
    sum_sc[n_blocks] = jnp.zeros((BS, width), F32)

    def add(p):
        code = pairs_ref[HALO_AT + p]
        b, h = code >> 2, code & 3
        rows = pl.ds(pl.multiple_of((h & (W - 1)) * BS, BS), BS)
        link = link_ref[:, rows, lanes.start - begin : lanes.stop - begin]
        v = jnp.where(h >= W, link, chip_ref[:, rows, lanes]).reshape(cols, width)
        sum_sc[b] += jnp.dot(weight_ref[p], v, preferred_element_type=F32)

    unrolled(pairs_ref[COUNT_AT + 1], add)
    for b in range(n_blocks):
        out_ref[b * BS : (b + 1) * BS, :] = sum_sc[b].astype(BF16)
    if lanes.start == 0:
        rest = stats_ref[...]
        for i in range(3):
            piece = rest.astype(BF16)
            rest = rest - piece.astype(F32)
            out_ref[pixels + i * 2 * n_blocks : pixels + (i + 1) * 2 * n_blocks, :] = piece


def unpack_stats(x, n_blocks):
    n = 2 * n_blocks
    x = x.astype(F32)
    x = (x[:n] + x[n : 2 * n]) + x[2 * n :]
    return x[:n_blocks], x[n_blocks:]


def combine(sizes, first_lane, count, *refs):
    frames, pixels, n_blocks, n_listed, key_width, value_width = sizes
    begin = first_lane == 0
    mine, other, refs = refs[:count], refs[count : 2 * count], refs[2 * count :]
    if begin:
        out_ref, cols_ref, out_sc, sem = refs
    else:
        cols_ref, before_ref, out_ref, out_sc, sem = refs

    def run(one, two):
        if begin:
            top_a, total_a = unpack_stats(one[0][pixels:, :], n_blocks)
            top_b, total_b = unpack_stats(two[0][pixels:, :], n_blocks)
            top = jnp.maximum(top_a, top_b)
            a, b = jnp.exp2(top_a - top), jnp.exp2(top_b - top)
            total = total_a * a + total_b * b
            a, b = a / total, b / total
        for i in range(n_blocks):
            r = slice(i * BS, (i + 1) * BS)
            if begin:
                cols_ref[0, r, :] = row_to_lanes(a[i : i + 1, :])
                cols_ref[1, r, :] = row_to_lanes(b[i : i + 1, :])
            for c in range(count):
                x = one[c][r, :].astype(F32) * cols_ref[0, r, :] + two[c][r, :].astype(F32) * cols_ref[1, r, :]
                out_sc[r, c * WIDTH : (c + 1) * WIDTH] = x.astype(BF16)

    me = lax.axis_index("tm")

    @pl.when(me == 0)
    def _():
        run(mine, other)

    @pl.when(me != 0)
    def _():
        run(other, mine)

    copy = pltpu.make_async_copy(out_sc, out_ref.at[:, pl.ds(first_lane, count * WIDTH)], sem)
    copy.start()
    copy.wait()


def shards(n_space, n_tm, query_key, selection, memory_key, shrinkage, memory_value, block_list, block_count):
    frames, pixels, key_width = memory_key.shape
    value_width = memory_value.shape[2]
    n_blocks, n_listed = block_list.shape
    sizes = (frames, pixels, n_blocks, n_listed, key_width, value_width)
    cols = frames * BS
    n_chunks = value_width // WIDTH
    link_rows = EDGE + W * key_width + 16
    chip_rows = EDGE + key_width + 16
    max_halo = n_blocks * min(n_listed, 2 * W) + UNROLL
    max_own = n_blocks * n_listed + UNROLL
    struct = jax.ShapeDtypeStruct
    dma = pltpu.SemaphoreType.DMA
    query, select = jnp.swapaxes(query_key[0], 0, 1), jnp.swapaxes(selection[0], 0, 1)
    keys = jnp.swapaxes(memory_key, 1, 2)
    query, select, keys, shrinkage, memory_value, block_list, block_count = [
        pltpu.with_memory_space_constraint(x, pltpu.HBM)
        for x in (query, select, keys, shrinkage, memory_value, block_list, block_count)
    ]
    on_chip = [(i ^ 1, i) for i in range(n_space)]
    over_link = []
    for i in range(n_space):
        for t in range(n_tm):
            j = i - 1 if i % 2 == 0 else i + 1
            source = j * n_tm + t if 0 <= j < n_space else i * n_tm + (t ^ 1)
            over_link.append((source, i * n_tm + t))
    round_link = [((i - 1 if i % 2 == 0 else i + 1) % n_space, i) for i in range(n_space)]
    swap = [(i ^ 1, i) for i in range(n_tm)]

    pairs, link_edge, chip_edge, cat, self_term, near_keys, near_shrink = pl.pallas_call(
        functools.partial(lists_and_edge, sizes),
        out_shape=(
            struct((256,), jnp.int32),
            struct((frames, link_rows, WIDTH), BF16),
            struct((frames, chip_rows, value_width), BF16),
            struct((n_blocks + 1, BS, 2 * key_width), BF16),
            struct((n_blocks + 1, BS, LANES), F32),
            struct((n_blocks, 2 * key_width, cols), BF16),
            struct((n_blocks, 1, cols), F32),
        ),
        in_specs=[HBM] * 7,
        out_specs=(SMEM,) + (VMEM,) * 6,
        scratch_shapes=[
            pltpu.SMEM(block_list.shape, jnp.int32),
            pltpu.SMEM(block_count.shape, jnp.int32),
            pltpu.VMEM(query.shape, BF16),
            pltpu.VMEM(select.shape, BF16),
            pltpu.VMEM(keys.shape, BF16),
            pltpu.VMEM(shrinkage.shape, BF16),
            dma((3,)),
            dma((W + 6,)),
        ],
        compiler_params=params(4),
        name="lists_and_edge",
    )(block_list, block_count, query, select, keys, shrinkage, memory_value)
    link_halo = [lax.ppermute(link_edge, ("space", "tm"), over_link)]
    chip_halo = lax.ppermute(chip_edge, "space", on_chip)

    acc, own_top, own_total, *more_edges = pl.pallas_call(
        functools.partial(own_part, sizes),
        out_shape=(
            struct((n_blocks + 1, BS, value_width), F32),
            struct((n_blocks + 1, BS, LANES), F32),
            struct((n_blocks + 1, BS, LANES), F32),
        )
        + (struct((frames, EDGE, WIDTH), BF16), struct((frames, EDGE, value_width - 2 * WIDTH), BF16)),
        in_specs=[SMEM, VMEM, VMEM, VMEM, VMEM, HBM],
        out_specs=(VMEM,) * 5,
        scratch_shapes=[
            pltpu.VMEM((max_own, BS, cols), F32),
            pltpu.VMEM(memory_value.shape, BF16),
            dma,
            dma((2,)),
        ],
        compiler_params=params(24),
        name="own_part",
    )(pairs, cat, self_term, near_keys, near_shrink, memory_value)
    def send_edge(axes, pairs, edge, *after):
        edge = pl.pallas_call(
            gate,
            out_shape=struct(edge.shape, edge.dtype),
            in_specs=[VMEM] * (1 + len(after)),
            out_specs=VMEM,
            input_output_aliases={0: 0},
            compiler_params=params(1),
            name="gate",
        )(edge, *after)
        return lax.ppermute(edge, axes, pairs)

    link_halo.append(send_edge(("space", "tm"), over_link, more_edges[0], own_top))

    weights, factor, stats = pl.pallas_call(
        functools.partial(halo_scores, sizes),
        out_shape=(
            struct((max_halo, BS, cols), BF16),
            struct((n_blocks + 1, BS, LANES), F32),
            struct((2 * n_blocks, LANES), F32),
        ),
        in_specs=[SMEM] + [VMEM] * 6,
        out_specs=(VMEM,) * 3,
        scratch_shapes=[
            pltpu.VMEM((2 * W, 2 * key_width, cols), BF16),
            pltpu.VMEM((2 * W, 1, cols), F32),
            pltpu.VMEM((max_halo, BS, cols), F32),
            pltpu.VMEM((n_blocks + 1, BS, LANES), F32),
            pltpu.VMEM((n_blocks + 1, BS, LANES), F32),
        ],
        compiler_params=params(12),
        cost_estimate=pl.CostEstimate(flops=30 * 10**9, bytes_accessed=2**20, transcendentals=0),
        name="halo_scores",
    )(pairs, cat, self_term, chip_halo, link_halo[0], own_top, own_total)

    cost = pl.CostEstimate(flops=30 * 10**9, bytes_accessed=2**20, transcendentals=0)
    mine, other = [], []
    for c in range(n_chunks):
        lanes = slice(c * WIDTH, (c + 1) * WIDTH)
        out_rows = pixels + (6 * n_blocks if c == 0 else 0)
        after = other[:1] if c >= 2 else []
        part = min(c, 2)
        begin = part * WIDTH
        x = pl.pallas_call(
            functools.partial(chunk_sums, sizes, lanes, begin),
            out_shape=struct((out_rows, WIDTH), BF16),
            in_specs=[SMEM] + [VMEM] * (6 + len(after)),
            out_specs=VMEM,
            scratch_shapes=[pltpu.VMEM((n_blocks + 1, BS, WIDTH), F32)],
            compiler_params=params(4),
            cost_estimate=cost if c == 1 else None,
            name=f"chunk_sums_{c}",
        )(pairs, weights, acc, factor, stats, chip_halo, link_halo[part], *after)
        mine.append(x)
        if c == 0:
            link_halo.append(send_edge("space", round_link, more_edges[1], x))
        other.append(lax.ppermute(x, "tm", swap) if n_tm == 2 else lax.all_gather(x, "tm"))

    if n_tm == 2:
        n = n_chunks - 1
        out, cols = pl.pallas_call(
            functools.partial(combine, sizes, 0, n),
            out_shape=(pltpu.HBM((pixels, value_width), BF16), struct((2, pixels, LANES), F32)),
            in_specs=[VMEM] * (2 * n),
            out_specs=(HBM, VMEM),
            scratch_shapes=[pltpu.VMEM((pixels, n * WIDTH), BF16), dma],
            compiler_params=params(2),
            name="combine_first",
        )(*mine[:n], *other[:n])
        out = pl.pallas_call(
            functools.partial(combine, sizes, n * WIDTH, 1),
            out_shape=pltpu.HBM((pixels, value_width), BF16),
            in_specs=[VMEM] * 3 + [HBM],
            out_specs=HBM,
            input_output_aliases={3: 0},
            scratch_shapes=[pltpu.VMEM((pixels, WIDTH), BF16), dma],
            compiler_params=params(2),
            name="combine_last",
        )(mine[n], other[n], cols, out)
    else:
        packed = other[0][:, pixels:, :]
        tops, totals = zip(*[unpack_stats(packed[i], n_blocks) for i in range(n_tm)])
        tops = jnp.stack(tops).reshape(n_tm, pixels, 1)
        totals = jnp.stack(totals).reshape(n_tm, pixels, 1)
        factors = jnp.exp2(tops - jnp.max(tops, axis=0, keepdims=True))
        total = jnp.sum(totals * factors, axis=0)
        sums = [jnp.sum(x[:, :pixels, :].astype(F32) * factors, axis=0) / total for x in other]
        out = jnp.concatenate(sums, axis=1).astype(BF16)
    return out[None]


def solution(mesh):
    in_specs = (
        P(None, "space", None),
        P(None, "space", None),
        P("tm", "space", None),
        P("tm", "space"),
        P("tm", "space", None),
        P("space", None),
        P("space"),
    )
    out_specs = P(None, "space", None)
    body = functools.partial(shards, mesh.shape["space"], mesh.shape["tm"])
    return jax.shard_map(body, mesh=mesh, in_specs=in_specs, out_specs=out_specs, check_vma=False)
```
